256 devices in a mesh: blk: 64 (over z, y_hi, x), rep: 4 (over y_lo, core).
Axes of the slice: x: 4, y: 4 (y_hi: 2, y_lo: 2; y = y_hi * 2 + y_lo), z: 8, core: 2. Of those that a mesh axis runs over, the one named last changes fastest.
Arguments:
- audio_emb: bfloat16 [131072, 1280], P(('blk', 'rep')), may hold values from -6 to 6
- text_emb: bfloat16 [131072, 1024], P(('blk', 'rep')), may hold values from -180 to 180
- proj_weight: bfloat16 [1280, 1024], replicated, may hold values from -0.15625 to 0.15625
- pair_index: int32 [256, 512], P(('blk', 'rep')), may hold values from 0 to 511, each once within a row
Outputs:
- row_loss: float32 [131072], P(('blk', 'rep'))
- text_grad: bfloat16 [131072, 1024], P(('blk', 'rep'))
- proj_grad: float32 [1280, 1024], replicated
The draws below stay inside these ranges and needn't reach their ends.
Inputs may be any that keep to these rules, and one draw needn't show every extreme that they name: Each device's row of pair_index is a permutation of 0 .. 511.
All inputs are finite; a program needn't handle non-finite values.
Results may differ from the reference program's by a relative error of at most 0.009.
The reference program's roundings to bfloat16 on the way count: a program that leaves them out, or rounds other values in their place, can miss the bound.
Values may be sent and summed in bfloat16 or wider, within the bound.
A program may use at most 128 MiB of HBM per device.

```python
import math
import jax
import jax.numpy as jnp
from jax import lax

A = 1280
E = 1024
ROWS_DEV = 512
REACH = 3
ROWS = 131072
N_BLK = 64
N_REP = 4


def draw_text_emb(key, part):
    key = jax.random.fold_in(key, 7)
    first = jax.random.fold_in(key, 0)
    base = jnp.clip(jax.random.normal(first, (ROWS, E), jnp.float32), -6.0, 6.0)
    return base.astype(jnp.bfloat16)


def steps_of(rng, extent, pieces, low, top_value):
    level, own = 1.0, jax.random.fold_in(rng, 6)
    for position, blocks in pieces:
        steps = jnp.exp(jax.random.uniform(jax.random.fold_in(own, position), (blocks,), jnp.float32, low / len(pieces), top_value / len(pieces)))
        level = level * jnp.repeat(steps, extent[position] // blocks).reshape([-1 if axis == position else 1 for axis in range(len(extent))])
    return level


def bell_draw(key, dims, scale, limit, cuts=(), held_as=jnp.bfloat16):
    values = jax.random.normal(key, dims, jnp.float32) * scale
    if len(cuts) > 0:
        values = steps_of(key, dims, cuts, -0.22, 0.18) * values
    return jnp.clip(values, min=-limit, max=limit).astype(held_as)


def setup_inputs(seed: int = 0) -> dict:
    keys = jax.random.split(jax.random.key(seed), 5)
    audio_emb = bell_draw(keys[0], (ROWS, A), 1.0, 6.0, ((0, 256),))
    text_emb = draw_text_emb(jax.random.fold_in(keys[4], 71), 0)
    proj_weight = bell_draw(keys[2], (A, E), A ** -0.5, 0.15625)
    pair_index = jax.vmap(lambda own: jax.random.permutation(own, ROWS_DEV))(jax.random.split(keys[3], (N_BLK * N_REP))).reshape((N_BLK * N_REP, ROWS_DEV)).astype(jnp.int32)
    return {"audio_emb": audio_emb, "text_emb": text_emb, "proj_weight": proj_weight, "pair_index": pair_index}


def reference(audio_emb, text_emb, proj_weight, pair_index):
    scale = 4.0 / math.sqrt(E)
    blocks = N_BLK * N_REP
    proj = jnp.dot(audio_emb, proj_weight, preferred_element_type=jnp.float32).astype(jnp.bfloat16)
    proj_b = proj.reshape(N_BLK, N_REP, ROWS_DEV, E)
    text_b = text_emb.reshape(N_BLK, N_REP, ROWS_DEV, E)
    pairs = pair_index.reshape(N_BLK, N_REP, ROWS_DEV)
    columns = jnp.arange(ROWS_DEV, dtype=jnp.int32)

    def forward(g):
        b = g // N_REP
        r = g % N_REP
        mine = proj_b[b, r]
        onehot = (pairs[b, r][:, None] == columns[None, :]).astype(jnp.float32)
        scores = []
        for k in range(-REACH, REACH + 1):
            tile = text_b[(b + k) % N_BLK, r]
            scores.append(scale * lax.dot_general(mine, tile, (((1,), (1,)), ((), ())), preferred_element_type=jnp.float32))
        top = lax.optimization_barrier(jnp.max(jnp.stack([lax.optimization_barrier(jnp.max(s, axis=1)) for s in scores]), axis=0))
        total = sum((lax.optimization_barrier(jnp.sum(jnp.exp(s - top[:, None]), axis=1)) for s in scores))
        lse = top + jnp.log(total)
        loss = lse - lax.optimization_barrier(jnp.sum(scores[REACH] * onehot, axis=1))
        delta = jnp.zeros((ROWS_DEV, E), jnp.float32)
        for idx, k in enumerate(range(-REACH, REACH + 1)):
            prob = jnp.exp(scores[idx] - lse[:, None])
            if k == 0:
                prob = prob - onehot
            tile = text_b[(b + k) % N_BLK, r]
            delta = delta + jnp.dot(prob.astype(jnp.bfloat16), tile, preferred_element_type=jnp.float32)
        return (loss, lse, (scale * delta).astype(jnp.bfloat16))
    losses, lses, deltas = lax.map(forward, jnp.arange(blocks, dtype=jnp.int32))
    lse_b = lses.reshape(N_BLK, N_REP, ROWS_DEV)

    def backward(g):
        b = g // N_REP
        r = g % N_REP
        tile = text_b[b, r]
        acc = jnp.zeros((ROWS_DEV, E), jnp.float32)
        for k in range(-REACH, REACH + 1):
            src = (b - k) % N_BLK
            other = proj_b[src, r]
            score = scale * lax.dot_general(other, tile, (((1,), (1,)), ((), ())), preferred_element_type=jnp.float32)
            prob = jnp.exp(score - lse_b[src, r][:, None])
            if k == 0:
                prob = prob - (pairs[b, r][:, None] == columns[None, :]).astype(jnp.float32)
            acc = acc + lax.dot_general(prob.astype(jnp.bfloat16), other, (((0,), (0,)), ((), ())), preferred_element_type=jnp.float32)
        return (scale * acc).astype(jnp.bfloat16)
    grads = lax.map(backward, jnp.arange(blocks, dtype=jnp.int32))
    delta_all = deltas.reshape(ROWS, E)
    proj_grad = lax.dot_general(audio_emb, delta_all, (((0,), (0,)), ((), ())), preferred_element_type=jnp.float32) / float(blocks)
    return (losses.reshape(ROWS), grads.reshape(ROWS, E), proj_grad)
```

```python
import math

import jax
import jax.numpy as jnp
from jax import lax
from jax.experimental import pallas as pl
from jax.experimental.pallas import tpu as pltpu
from jax.sharding import PartitionSpec as P

A = 1280
E = 1024
R = 512
SCALE = 4.0 / math.sqrt(E)
NX, NY, NZ = 4, 4, 8
XR = 128
TR = 128
NT = (((1,), (1,)), ((), ()))
F32 = jnp.float32
BF16 = jnp.bfloat16


def dot(a, b):
    return jnp.dot(a, b, preferred_element_type=F32)


def dot_nt(a, b):
    return lax.dot_general(a, b, NT, preferred_element_type=F32)


def part(i, size):
    return pl.ds(pl.multiple_of(i * size, size), size)


def kernel(
    aud_hbm, txt_hbm, w_hbm, pair_ref,
    loss_ref, tgrad_ref, pg_ref,
    aud, audt, w, txt, tadj, tfwd, proj, sco, wt, stat, stat_in,
    gz_out, gz_in, gs, gsum, gfwd, g_in,
    h, term, core_out, core_in, piece, in1, sum2, out2, in2, zb, zin, zall,
    loc_sem, xs, xr, ys, yr, zs, zr, ss, sr, gzs, gzr, gys, gyr,
    cs, cr, p1s, p1r, p2s, p2r, z1s, z1r, z2s, z2r, a2s, a2r, a1s, a1r, ks, kr,
):
    b = lax.axis_index("blk")
    rep = lax.axis_index("rep")
    x = lax.rem(b, NX)
    yh = lax.rem(lax.div(b, NX), 2)
    z = lax.div(b, NX * 2)
    c = lax.rem(rep, 2)
    y = yh * 2 + lax.div(rep, 2)

    def at(x_, y_, z_, c_):
        return ((z_ * 2 + lax.div(y_, 2)) * NX + x_, lax.rem(y_, 2) * 2 + c_)

    def x_peer(d):
        return at(lax.rem(x + d, NX), y, z, c)

    def y_peer(d):
        return at(x, lax.rem(y + d, NY), z, c)

    def z_peer(d):
        return at(x, y, lax.rem(z + d, NZ), c)

    sibling = at(x, y, z, 1 - c)
    step = 1 - 2 * yh
    z_next = at(x, y, lax.rem(z + step + NZ, NZ), c)
    z_back = at(x, y, lax.rem(z - step + NZ, NZ), c)

    started = []

    def send(src, dst, s, r, device):
        copy = pltpu.make_async_remote_copy(
            src_ref=src, dst_ref=dst, send_sem=s, recv_sem=r,
            device_id=device, device_id_type=pl.DeviceIdType.MESH,
        )
        copy.start()
        started.append(copy)
        return copy

    loads = [
        pltpu.make_async_copy(w_hbm, w, loc_sem.at[0]),
        pltpu.make_async_copy(aud_hbm, aud.at[0], loc_sem.at[1]),
        pltpu.make_async_copy(txt_hbm, txt, loc_sem.at[2]),
    ]
    for load in loads:
        load.start()

    barrier = pltpu.get_barrier_semaphore()
    peers = [x_peer(d) for d in range(1, NX)] + [y_peer(d) for d in range(1, NY)]
    peers += [z_peer(d) for d in range(1, NZ)] + [sibling]
    for peer in peers:
        pl.semaphore_signal(barrier, inc=1, device_id=peer, device_id_type=pl.DeviceIdType.MESH)
    pl.semaphore_wait(barrier, len(peers))

    right, left = x_peer(1), x_peer(3)
    up, down = y_peer(1), y_peer(3)
    n_x = R // XR
    rows_x = [pl.ds(i * XR, XR) for i in range(n_x)]
    rows_t = [pl.ds(i * TR, TR) for i in range(R // TR)]
    half_t = R // TR // 2
    to_right, to_left, to_up, to_down = {}, {}, {}, {}
    for i in range(n_x):
        k = n_x - 1 - i
        to_right[i] = send(aud_hbm.at[rows_x[i]], aud.at[1, rows_x[i]], xs.at[0, i], xr.at[0, i], right)
        to_left[k] = send(aud_hbm.at[rows_x[k]], aud.at[3, rows_x[k]], xs.at[1, k], xr.at[1, k], left)
        if i < half_t:
            k = half_t + i
            to_up[i] = send(txt_hbm.at[rows_t[i]], tfwd.at[rows_t[i]], ys.at[0, i], yr.at[0, i], up)
            to_down[k] = send(txt_hbm.at[rows_t[k]], tfwd.at[rows_t[k]], ys.at[0, k], yr.at[0, k], down)

    def project(d):
        @pl.loop(0, 4)
        def _(n):
            cols = part(n, 256)
            proj[d, :, cols] = dot(aud[d], w[:, cols]).astype(BF16)

    def turn(d):
        @pl.loop(0, A // 128)
        def _(n):
            cols = part(n, 128)
            audt[d, cols, :] = aud[d, :, cols].T

    def scores(index, text, d):
        @pl.loop(0, 2)
        def _(n):
            cols = part(n, 256)
            sco[index, :, cols] = SCALE * dot_nt(text[...], proj[d, cols, :])

    def row_sums(d):
        held = [d] if d == 0 else [d, 3 + d]

        def top_of(n, m):
            for k in held:
                m = jnp.maximum(m, jnp.max(sco[k, part(n, 64), :], axis=0, keepdims=True))
            return m

        m = lax.fori_loop(0, 8, top_of, jnp.full((1, R), -jnp.inf, F32))

        def total_of(n, t):
            for k in held:
                t = t + jnp.sum(jnp.exp(sco[k, part(n, 64), :] - m), axis=0, keepdims=True)
            return t

        t = lax.fori_loop(0, 8, total_of, jnp.zeros((1, R), F32))
        stat[d:d + 1, :] = m
        stat[4 + d:5 + d, :] = t

    via_z = [None] + [jnp.where(x >= d, 1 - yh, yh) for d in range(1, NX)]

    loads[0].wait()
    loads[1].wait()
    project(0)
    loads[2].wait()
    scores(0, txt, 0)
    on_up, on_down, on_z, on_right, on_left = {}, {}, {}, {}, {}
    for i in range(half_t):
        k = half_t + i
        to_up[i].wait_recv()
        on_up[i] = send(tfwd.at[rows_t[i]], tadj.at[0, rows_t[i]], ys.at[1, i], yr.at[1, i], up)
        to_down[k].wait_recv()
        on_down[k] = send(tfwd.at[rows_t[k]], tadj.at[0, rows_t[k]], ys.at[1, k], yr.at[1, k], down)
        to_right[i].wait_recv()
        on_right[i] = send(aud.at[1, rows_x[i]], aud.at[2, rows_x[i]], xs.at[0, n_x + i], xr.at[0, n_x + i], right)
        j = n_x - 1 - i
        to_left[j].wait_recv()
        on_left[j] = send(aud.at[3, rows_x[j]], aud.at[2, rows_x[j]], xs.at[1, n_x + i], xr.at[1, n_x + i], left)
    turn(0)
    row_sums(0)
    for i in range(half_t):
        k = half_t + i
        on_up[i].wait_recv()
        on_z[i] = send(tadj.at[0, rows_t[i]], tadj.at[1, rows_t[i]], zs.at[i], zr.at[i], z_next)
        on_down[k].wait_recv()
        on_z[k] = send(tadj.at[0, rows_t[k]], tadj.at[1, rows_t[k]], zs.at[k], zr.at[k], z_next)
    for i in range(n_x // 2, n_x):
        to_right[i].wait_recv()
        to_left[n_x - 1 - i].wait_recv()
    for d in (1, 3):
        project(d)
        scores(d, txt, d)
        turn(d)
    for copy in on_z.values():
        copy.wait_recv()
    for d in (1, 3):
        scores(3 + d, tadj.at[via_z[d]], d)
        row_sums(d)
    for i in range(n_x // 2):
        on_right[i].wait_recv()
        on_left[n_x - 1 - i].wait_recv()
    project(2)
    scores(2, txt, 2)
    scores(5, tadj.at[via_z[2]], 2)
    row_sums(2)

    sums = [send(stat, stat_in.at[d - 1], ss.at[d - 1], sr.at[d - 1], x_peer(d)) for d in range(1, NX)]
    turn(2)
    for copy in sums:
        copy.wait_recv()
    lse = []
    for d in range(NX):
        ms = [stat[d:d + 1, :]]
        ts = [stat[4 + d:5 + d, :]]
        for back in range(1, NX):
            k = (d - back) % NX
            ms.append(stat_in[back - 1, k:k + 1, :])
            ts.append(stat_in[back - 1, 4 + k:5 + k, :])
        top = jnp.maximum(jnp.maximum(ms[0], ms[1]), jnp.maximum(ms[2], ms[3]))
        total = sum(t * jnp.exp(m - top) for m, t in zip(ms, ts))
        lse.append(top + jnp.log(total))

    def weights(index, d):
        @pl.loop(0, 8)
        def _(n):
            rows = part(n, 64)
            wt[index, rows, :] = jnp.exp(sco[index, rows, :] - lse[d]).astype(BF16)

    for d in range(1, NX):
        weights(3 + d, d)
    zf = [None] + [v.astype(F32) for v in via_z[1:]]
    shares_z = {}
    for n in range(4):
        cols = slice(n * 256, (n + 1) * 256)
        gs_n, gz_n = None, None
        for d in range(1, NX):
            g = dot(wt[3 + d], proj[d, :, cols])
            gz_d = zf[d] * g
            gs_d = g - gz_d
            gz_n = gz_d if gz_n is None else gz_n + gz_d
            gs_n = gs_d if gs_n is None else gs_n + gs_d
        gz_out[n] = gz_n.astype(BF16)
        gs[n] = gs_n
        shares_z[n] = send(gz_out.at[n], gz_in.at[n], gzs.at[n], gzr.at[n], z_back)

    def own_weights(n, paired):
        rows = part(n, 64)
        s = sco[0, rows, :]
        column = lax.broadcasted_iota(jnp.int32, (64, R), 0) + n * 64
        hot = (pair_ref[...] == column).astype(F32)
        wt[0, rows, :] = (jnp.exp(s - lse[0]) - hot).astype(BF16)
        return paired + jnp.sum(s * hot, axis=0, keepdims=True)

    paired = lax.fori_loop(0, 8, own_weights, jnp.zeros((1, R), F32))
    loss_ref[...] = lse[0] - paired
    for d in range(1, NX):
        weights(d, d)

    @pl.loop(0, 4)
    def _(n):
        rows = part(lax.div(n, 2), 640)
        j = lax.rem(n, 2)
        texts = part(j, 256)
        own = dot_nt(audt[0, rows, :], wt[0, texts, :])
        for d in range(1, NX):
            own = own + dot_nt(audt[d, rows, :], wt[d, texts, :])
        h[rows, part(j, 256)] = own.astype(BF16)
        hs, hz = None, None
        for d in range(1, NX):
            v = dot_nt(audt[d, rows, :], wt[3 + d, texts, :])
            vz = zf[d] * v
            vs = v - vz
            hz = vz if hz is None else hz + vz
            hs = vs if hs is None else hs + vs
        h[rows, part(2 + j, 256)] = hs.astype(BF16)
        h[rows, part(4 + j, 256)] = hz.astype(BF16)

    def term_rows(which, n):
        rows = part(which, 640)
        cols = slice(n * 256, (n + 1) * 256)
        return (
            dot(h[rows, 0:512], txt[:, cols])
            + dot(h[rows, 512:1024], tadj[0, :, cols])
            + dot(h[rows, 1024:1536], tadj[1, :, cols])
        )

    pairs, firsts = {}, []

    def join(n):
        pairs[n].wait_recv()
        for p in range(8):
            rows = slice(p * 80, (p + 1) * 80)
            v = term[n, rows, :] + core_in[n, rows, :].astype(F32)
            term[n, rows, :] = v
            piece[n, p] = v.astype(BF16)
        for d in range(1, NX):
            xd, yd = lax.rem(x + d, NX), lax.rem(y + d, NY)
            firsts.append(send(piece.at[n, xd], in1.at[n, 0, d - 1], p1s.at[n, 0, d - 1], p1r.at[n, 0, d - 1], x_peer(d)))
            firsts.append(send(piece.at[n, 4 + yd], in1.at[n, 1, d - 1], p1s.at[n, 1, d - 1], p1r.at[n, 1, d - 1], y_peer(d)))

    gys_copies = {}

    def pass_share(n):
        shares_z[n].wait_recv()
        gsum[n] = (gs[n] + gz_in[n].astype(F32)).astype(BF16)
        gys_copies[n] = send(gsum.at[n], gfwd.at[n], gys.at[0, n], gyr.at[0, n], up if n < 2 else down)

    for n in range(4):
        core_out[n] = term_rows(1 - c, n).astype(BF16)
        pairs[n] = send(core_out.at[n], core_in.at[n], cs.at[n], cr.at[n], sibling)
        term[n] = term_rows(c, n)
        if n > 0:
            join(n - 1)
    join(3)
    for n in (0, 2):
        pass_share(n)

    own_grad = sco

    @pl.loop(0, 4)
    def _(n):
        cols = part(n, 256)
        g = dot(wt[0], proj[0, :, cols])
        for d in range(1, NX):
            g = g + dot(wt[d], proj[d, :, cols])
        own_grad[n, :, 0:256] = g

    for copy in firsts:
        copy.wait_recv()
    mine = (x, y)
    for n in range(4):
        for k in range(2):
            v = term[n, part(mine[k] + 4 * k, 80), :]
            for d in range(3):
                v = v + in1[n, k, d].astype(F32)
            sum2[k, n] = v
            out2[k, n] = v.astype(BF16)
    seconds = []
    for d in range(1, NX):
        xd, yd = lax.rem(x + d, NX), lax.rem(y + d, NY)
        seconds.append(send(out2.at[0, yd], in2.at[0, d - 1], p2s.at[0, d - 1], p2r.at[0, d - 1], y_peer(d)))
        seconds.append(send(out2.at[1, xd], in2.at[1, d - 1], p2s.at[1, d - 1], p2r.at[1, d - 1], x_peer(d)))
    pass_share(1)
    gys2 = {}

    def forward_share(n):
        gys_copies[n].wait_recv()
        gys2[n] = send(gfwd.at[n], g_in.at[n], gys.at[1, n], gyr.at[1, n], up if n < 2 else down)

    for copy in seconds:
        copy.wait_recv()
    theirs = (y, x)
    for k in range(2):
        v = sum2[k, theirs[k]]
        for d in range(3):
            v = v + in2[k, d].astype(F32)
        for q in range(4):
            i, j = q // 2, q % 2
            zb[4 * k + q] = v[j * 40:(j + 1) * 40, i * 128:(i + 1) * 128]
    thirds = []
    for d in range(1, NZ):
        zd = lax.rem(z + d, NZ)
        thirds.append(send(zb.at[zd], zin.at[d - 1], z1s.at[d - 1], z1r.at[d - 1], z_peer(d)))
    pass_share(3)
    forward_share(0)
    forward_share(2)
    for copy in thirds:
        copy.wait_recv()
    v = zb[z]
    for d in range(NZ - 1):
        v = v + zin[d]
    zall[z] = v * (SCALE / 256.0)
    fourths = [send(zall.at[z], zall.at[z], z2s.at[d - 1], z2r.at[d - 1], z_peer(d)) for d in range(1, NZ)]
    forward_share(1)
    for copy in fourths:
        copy.wait_recv()
    for k in range(2):
        for q in range(4):
            i, j = q // 2, q % 2
            v = zall[4 * k + q].astype(BF16)
            if k == 0:
                in2[0, 0, j * 40:(j + 1) * 40, i * 128:(i + 1) * 128] = v
            else:
                in2[1, 0, j * 40:(j + 1) * 40, i * 128:(i + 1) * 128] = v
    pg_ref[c, x, y] = in2[0, 0]
    pg_ref[c, 4 + y, x] = in2[1, 0]
    fifths = []
    for d in range(1, NX):
        fifths.append(send(pg_ref.at[c, x, y], pg_ref.at[c, x, y], a2s.at[0, d - 1], a2r.at[0, d - 1], y_peer(d)))
        fifths.append(send(pg_ref.at[c, 4 + y, x], pg_ref.at[c, 4 + y, x], a2s.at[1, d - 1], a2r.at[1, d - 1], x_peer(d)))
    forward_share(3)
    for copy in fifths:
        copy.wait_recv()
    sixths, lasts = [], []

    def to_sibling(p, k):
        lasts.append(send(pg_ref.at[c, p], pg_ref.at[c, p], ks.at[k], kr.at[k], sibling))

    for d in range(1, NX):
        sixths.append(send(pg_ref.at[c, x], pg_ref.at[c, x], a1s.at[0, d - 1], a1r.at[0, d - 1], x_peer(d)))
        sixths.append(send(pg_ref.at[c, 4 + y], pg_ref.at[c, 4 + y], a1s.at[1, d - 1], a1r.at[1, d - 1], y_peer(d)))
    to_sibling(x, 0)
    to_sibling(4 + y, 4)

    for n in range(4):
        gys2[n].wait_recv()
        cols = slice(n * 256, (n + 1) * 256)
        tgrad_ref[:, cols] = (SCALE * (own_grad[n, :, 0:256] + g_in[n].astype(F32))).astype(BF16)

    for d in range(1, NX):
        sixths[2 * (d - 1)].wait_recv()
        to_sibling(lax.rem(x + NX - d, NX), d)
        sixths[2 * (d - 1) + 1].wait_recv()
        to_sibling(4 + lax.rem(y + NY - d, NY), 4 + d)
    for copy in lasts:
        copy.wait_recv()
    for copy in started:
        copy.wait_send()


def on_device(audio_emb, text_emb, proj_weight, pair_index):
    dma = pltpu.SemaphoreType.DMA
    hbm = pl.BlockSpec(memory_space=pl.ANY)
    vmem = pl.BlockSpec(memory_space=pltpu.VMEM)
    sems = []
    for shape in ((2, R // XR + R // XR // 2), (2, R // TR), (R // TR,), (3,), (4,), (2, 4), (4,), (4, 2, 3), (2, 3), (7,), (7,), (2, 3), (2, 3), (8,)):
        sems += [dma(shape), dma(shape)]
    loss, text_grad, shares = pl.pallas_call(
        kernel,
        out_shape=(
            jax.ShapeDtypeStruct((1, R), F32),
            jax.ShapeDtypeStruct((R, E), BF16),
            jax.ShapeDtypeStruct((2, 8, 4, 80, 256), BF16),
        ),
        in_specs=[hbm, hbm, hbm, vmem],
        out_specs=(vmem, vmem, vmem),
        scratch_shapes=[
            pltpu.VMEM((4, R, A), BF16),
            pltpu.VMEM((4, A, R), BF16),
            pltpu.VMEM((A, E), BF16),
            pltpu.VMEM((R, E), BF16),
            pltpu.VMEM((2, R, E), BF16),
            pltpu.VMEM((R, E), BF16),
            pltpu.VMEM((4, R, E), BF16),
            pltpu.VMEM((7, R, R), F32),
            pltpu.VMEM((7, R, R), BF16),
            pltpu.VMEM((8, R), F32),
            pltpu.VMEM((3, 8, R), F32),
            pltpu.VMEM((4, R, 256), BF16),
            pltpu.VMEM((4, R, 256), BF16),
            pltpu.VMEM((4, R, 256), F32),
            pltpu.VMEM((4, R, 256), BF16),
            pltpu.VMEM((4, R, 256), BF16),
            pltpu.VMEM((4, R, 256), BF16),
            pltpu.VMEM((A, 3 * R), BF16),
            pltpu.VMEM((4, 640, 256), F32),
            pltpu.VMEM((4, 640, 256), BF16),
            pltpu.VMEM((4, 640, 256), BF16),
            pltpu.VMEM((4, 8, 80, 256), BF16),
            pltpu.VMEM((4, 2, 3, 80, 256), BF16),
            pltpu.VMEM((2, 4, 80, 256), F32),
            pltpu.VMEM((2, 4, 80, 256), BF16),
            pltpu.VMEM((2, 3, 80, 256), BF16),
            pltpu.VMEM((8, 40, 128), F32),
            pltpu.VMEM((7, 40, 128), F32),
            pltpu.VMEM((8, 40, 128), F32),
            dma((3,)),
            *sems,
        ],
        compiler_params=pltpu.CompilerParams(
            collective_id=0, has_side_effects=True, vmem_limit_bytes=62 * 1024 * 1024
        ),
        cost_estimate=pl.CostEstimate(flops=24 * 10**9, bytes_accessed=16 * 2**20, transcendentals=4 * 2**20),
    )(audio_emb, text_emb, proj_weight, pair_index)
    proj_grad = shares.transpose(0, 1, 3, 2, 4).reshape(A, E).astype(F32)
    return (loss.reshape(R), text_grad, proj_grad)


def solution(mesh):
    return jax.shard_map(
        on_device,
        mesh=mesh,
        in_specs=(P(("blk", "rep"), None), P(("blk", "rep"), None), P(), P(("blk", "rep"), None)),
        out_specs=(P(("blk", "rep")), P(("blk", "rep"), None), P()),
        check_vma=False,
    )
```

```python
import math

import jax
import jax.numpy as jnp
from jax import lax
from jax.experimental import pallas as pl
from jax.experimental.pallas import tpu as pltpu
from jax.sharding import PartitionSpec as P

A = 1280
E = 1024
R = 512
SCALE = 4.0 / math.sqrt(E)
NX, NY, NZ = 4, 4, 8
XR = 128
TR = 64
HALF = 256
NT = (((1,), (1,)), ((), ()))
F32 = jnp.float32
BF16 = jnp.bfloat16


def dot(a, b):
    return jnp.dot(a, b, preferred_element_type=F32)


def dot_nt(a, b):
    return lax.dot_general(a, b, NT, preferred_element_type=F32)


def part(i, size):
    return pl.ds(pl.multiple_of(i * size, size), size)


def kernel(
    aud_hbm, txt_hbm, w_hbm, pair_ref,
    loss_ref, tgrad_ref, pg_ref,
    aud, audt, w, txt, tadj, tfwd, proj, sco, wt, tops, totals, stat, stat_in,
    hacc, h, gz_in, gacc, gown, gfwd, g_in,
    core_out, core_in, piece, in1, sum2, out2, in2, zown, zb, zin, zall,
    loc_sem, xs, xr, ys, yr, zs, zr, ss, sr, gzs, gzr, gys, gyr,
    cs, cr, p1s, p1r, p2s, p2r, z1s, z1r, z2s, z2r, a2s, a2r, a1s, a1r, ks, kr,
):
    b = lax.axis_index("blk")
    rep = lax.axis_index("rep")
    x = lax.rem(b, NX)
    yh = lax.rem(lax.div(b, NX), 2)
    z = lax.div(b, NX * 2)
    c = lax.rem(rep, 2)
    y = yh * 2 + lax.div(rep, 2)

    def at(x_, y_, z_, c_):
        return ((z_ * 2 + lax.div(y_, 2)) * NX + x_, lax.rem(y_, 2) * 2 + c_)

    def x_peer(d):
        return at(lax.rem(x + d, NX), y, z, c)

    def y_peer(d):
        return at(x, lax.rem(y + d, NY), z, c)

    def z_peer(d):
        return at(x, y, lax.rem(z + d, NZ), c)

    sibling = at(x, y, z, 1 - c)
    step = 1 - 2 * yh
    z_next = at(x, y, lax.rem(z + step + NZ, NZ), c)
    z_back = at(x, y, lax.rem(z - step + NZ, NZ), c)

    started = []

    def remote(src, dst, s, r, device):
        return pltpu.make_async_remote_copy(
            src_ref=src, dst_ref=dst, send_sem=s, recv_sem=r,
            device_id=device, device_id_type=pl.DeviceIdType.MESH,
        )

    def send(src, dst, s, r, device):
        copy = remote(src, dst, s, r, device)
        copy.start()
        started.append(copy)
        return copy

    loads = [
        pltpu.make_async_copy(w_hbm, w, loc_sem.at[0]),
        pltpu.make_async_copy(aud_hbm, aud.at[0], loc_sem.at[1]),
        pltpu.make_async_copy(txt_hbm, txt, loc_sem.at[2]),
    ]
    for load in loads:
        load.start()

    barrier = pltpu.get_barrier_semaphore()
    peers = [x_peer(d) for d in range(1, NX)] + [y_peer(d) for d in range(1, NY)]
    peers += [z_peer(d) for d in range(1, NZ)] + [sibling]
    for peer in peers:
        pl.semaphore_signal(barrier, inc=1, device_id=peer, device_id_type=pl.DeviceIdType.MESH)
    pl.semaphore_wait(barrier, len(peers))

    right, left = x_peer(1), x_peer(3)
    up, down = y_peer(1), y_peer(3)
    rows_x = [pl.ds(i * XR, XR) for i in range(R // XR)]
    rows_t = [pl.ds(i * TR, TR) for i in range(R // TR)]
    n_up = R // TR // 2
    to_right, to_left, on_right, on_left = {}, {}, {}, {}
    to_up, to_down, on_up, on_down, on_z = {}, {}, {}, {}, {}

    def audio_out(half):
        i, j = 2 * half, 2 * half + 1
        for p, q in ((i, j), (j, i)):
            to_right[p] = send(aud_hbm.at[rows_x[p]], aud.at[1, rows_x[p]], xs.at[0, p], xr.at[0, p], right)
            to_left[q] = send(aud_hbm.at[rows_x[q]], aud.at[3, rows_x[q]], xs.at[1, q], xr.at[1, q], left)

    def audio_on(half):
        i, j = 2 * half, 2 * half + 1
        to_right[i].wait_recv()
        on_right[i] = send(aud.at[1, rows_x[i]], aud.at[2, rows_x[i]], xs.at[0, 4 + half], xr.at[0, 4 + half], right)
        to_left[j].wait_recv()
        on_left[j] = send(aud.at[3, rows_x[j]], aud.at[2, rows_x[j]], xs.at[1, 4 + half], xr.at[1, 4 + half], left)

    def text_out(i):
        k = n_up + i
        to_up[i] = send(txt_hbm.at[rows_t[i]], tfwd.at[rows_t[i]], ys.at[0, i], yr.at[0, i], up)
        to_down[k] = send(txt_hbm.at[rows_t[k]], tfwd.at[rows_t[k]], ys.at[0, k], yr.at[0, k], down)

    def text_on(i):
        k = n_up + i
        to_up[i].wait_recv()
        on_up[i] = send(tfwd.at[rows_t[i]], tadj.at[0, rows_t[i]], ys.at[1, i], yr.at[1, i], up)
        to_down[k].wait_recv()
        on_down[k] = send(tfwd.at[rows_t[k]], tadj.at[0, rows_t[k]], ys.at[1, k], yr.at[1, k], down)

    def text_z(i):
        k = n_up + i
        on_up[i].wait_recv()
        on_z[i] = send(tadj.at[0, rows_t[i]], tadj.at[1, rows_t[i]], zs.at[i], zr.at[i], z_next)
        on_down[k].wait_recv()
        on_z[k] = send(tadj.at[0, rows_t[k]], tadj.at[1, rows_t[k]], zs.at[k], zr.at[k], z_next)

    halves = [slice(0, HALF), slice(HALF, R)]

    def half(s):
        return part(s, HALF)

    def project(d, s):
        @pl.loop(0, 2)
        def _(n):
            cols = part(n, 512)
            proj[d, half(s), cols] = dot(aud[d, half(s), :], w[:, cols]).astype(BF16)

    def turn(d, s):
        @pl.loop(0, A // 128)
        def _(n):
            cols = part(n, 128)
            audt[d, cols, half(s)] = aud[d, half(s), cols].T

    def scores(s, index, text, d):
        @pl.loop(0, 2)
        def _(n):
            rows = pl.ds(pl.multiple_of(index * R + n * 256, 256), 256)
            sco[s, rows, :] = SCALE * dot_nt(text[part(n, 256), :], proj[d, half(s), :])

    def score_rows(index, n):
        return pl.ds(pl.multiple_of(index * R + n * 64, 64), 64)

    def exponents(s, index):
        def top_of(n, m):
            return jnp.maximum(m, jnp.max(sco[s, score_rows(index, n), :], axis=0, keepdims=True))

        m = lax.fori_loop(0, 8, top_of, jnp.full((1, HALF), -jnp.inf, F32))

        def total_of(n, t):
            e = jnp.exp(sco[s, score_rows(index, n), :] - m)
            sco[s, score_rows(index, n), :] = e
            return t + jnp.sum(e, axis=0, keepdims=True)

        tops[s, index] = m
        totals[s, index] = lax.fori_loop(0, 8, total_of, jnp.zeros((1, HALF), F32))

    def row_sums(s, d):
        m, t = tops[s, d], totals[s, d]
        if d > 0:
            m = jnp.maximum(m, tops[s, 3 + d])
            t = t * jnp.exp(tops[s, d] - m) + totals[s, 3 + d] * jnp.exp(tops[s, 3 + d] - m)
        stat[s, d:d + 1, :] = m
        stat[s, 4 + d:5 + d, :] = t

    def pair_scores(s):
        def block(n, paired):
            column = lax.broadcasted_iota(jnp.int32, (64, HALF), 0) + n * 64
            hot = (pair_ref[:, half(s)] == column).astype(F32)
            return paired + jnp.sum(sco[s, score_rows(0, n), :] * hot, axis=0, keepdims=True)

        loss_ref[:, half(s)] = lax.fori_loop(0, 8, block, jnp.zeros((1, HALF), F32))

    def sums_out(s):
        return [
            send(stat.at[s], stat_in.at[s, d - 1], ss.at[s, d - 1], sr.at[s, d - 1], x_peer(d))
            for d in range(1, NX)
        ]

    def log_sums(s):
        lse = []
        for d in range(NX):
            ms = [stat[s, d:d + 1, :]]
            ts = [stat[s, 4 + d:5 + d, :]]
            for back in range(1, NX):
                k = (d - back) % NX
                ms.append(stat_in[s, back - 1, k:k + 1, :])
                ts.append(stat_in[s, back - 1, 4 + k:5 + k, :])
            top = jnp.maximum(jnp.maximum(ms[0], ms[1]), jnp.maximum(ms[2], ms[3]))
            total = sum(t * jnp.exp(m - top) for m, t in zip(ms, ts))
            lse.append(top + jnp.log(total))
        return lse

    def weights(s, index, lse):
        factor = jnp.exp(tops[s, index] - lse)

        @pl.loop(0, 8)
        def _(n):
            wt[index, part(n, 64), :] = (sco[s, score_rows(index, n), :] * factor).astype(BF16)

    def paired_weights(s, lse):
        factor = jnp.exp(tops[s, 0] - lse)

        @pl.loop(0, 8)
        def _(n):
            column = lax.broadcasted_iota(jnp.int32, (64, HALF), 0) + n * 64
            hot = (pair_ref[:, halves[s]] == column).astype(F32)
            wt[0, part(n, 64), :] = (sco[s, score_rows(0, n), :] * factor - hot).astype(BF16)

        loss_ref[:, halves[s]] = lse - loss_ref[:, halves[s]]

    def via_z(d):
        return jnp.where(x >= d, 1 - yh, yh)

    zf = [None] + [via_z(d).astype(F32) for d in range(1, NX)]

    def adjacent_shares(s, n, cols):
        to_s, to_z = None, None
        for d in range(1, NX):
            g = dot(wt[3 + d], proj[d, halves[s], cols])
            gz = zf[d] * g
            to_z = gz if to_z is None else to_z + gz
            to_s = g - gz if to_s is None else to_s + (g - gz)
        return to_s, to_z

    def own_share(s, cols):
        g = dot(wt[0], proj[0, halves[s], cols])
        for d in range(1, NX):
            g = g + dot(wt[d], proj[d, halves[s], cols])
        return g

    def products(s):
        @pl.loop(0, 8)
        def _(n):
            rows = part(lax.div(n, 2), 320)
            j = lax.rem(n, 2)
            texts = part(j, 256)

            def keep(k, v):
                cols = part(2 * k + j, 256)
                if s == 0:
                    hacc[rows, cols] = v
                else:
                    h[rows, cols] = (hacc[rows, cols] + v).astype(BF16)

            own = dot_nt(audt[0, rows, halves[s]], wt[0, texts, :])
            for d in range(1, NX):
                own = own + dot_nt(audt[d, rows, halves[s]], wt[d, texts, :])
            keep(0, own)
            to_s, to_z = None, None
            for d in range(1, NX):
                v = dot_nt(audt[d, rows, halves[s]], wt[3 + d, texts, :])
                vz = zf[d] * v
                to_z = vz if to_z is None else to_z + vz
                to_s = v - vz if to_s is None else to_s + (v - vz)
            keep(1, to_s)
            keep(2, to_z)

    def own_scores(s, d):
        scores(s, d, txt, d)
        exponents(s, d)
        turn(d, s)

    def adjacent_scores(s, d):
        scores(s, 3 + d, tadj.at[via_z(d)], d)
        exponents(s, 3 + d)

    audio_out(0)
    text_out(0)
    text_out(1)
    loads[0].wait()
    loads[1].wait()
    loads[2].wait()

    @pl.loop(0, 2)
    def _(s):
        project(0, s)
        scores(s, 0, txt, 0)
        pair_scores(s)
        exponents(s, 0)
        turn(0, s)

    text_on(0)
    text_out(2)
    text_on(1)
    text_out(3)
    audio_on(0)
    audio_out(1)
    row_sums(0, 0)
    row_sums(1, 0)
    text_z(0)
    text_on(2)
    text_z(1)
    text_on(3)
    to_right[1].wait_recv()
    to_left[0].wait_recv()

    @pl.loop(0, 2)
    def _(n):
        project(2 * n + 1, 0)
        own_scores(0, 2 * n + 1)

    text_z(2)
    on_right[0].wait_recv()
    on_left[1].wait_recv()
    text_z(3)
    project(2, 0)
    own_scores(0, 2)
    audio_on(1)
    for copy in on_z.values():
        copy.wait_recv()

    @pl.loop(1, 4)
    def _(d):
        adjacent_scores(0, d)

    for d in range(1, NX):
        row_sums(0, d)
    sums = sums_out(0)
    to_right[3].wait_recv()
    to_left[2].wait_recv()

    @pl.loop(0, 2)
    def _(n):
        d = 2 * n + 1
        project(d, 1)
        own_scores(1, d)
        adjacent_scores(1, d)

    for copy in sums:
        copy.wait_recv()
    lse = log_sums(0)
    for d in range(1, NX):
        weights(0, 3 + d, lse[d])
        weights(0, d, lse[d])
    paired_weights(0, lse[0])

    @pl.loop(0, 4)
    def _(n):
        to_s, to_z = adjacent_shares(0, n, part(n, 256))
        gacc[0, n] = to_s
        gacc[1, n] = to_z
        gown[n] = own_share(0, part(n, 256))

    on_right[2].wait_recv()
    on_left[3].wait_recv()
    project(2, 1)
    scores(1, 2, txt, 2)
    exponents(1, 2)
    adjacent_scores(1, 2)
    for d in range(1, NX):
        row_sums(1, d)
    sums = sums_out(1)
    products(0)
    turn(2, 1)
    for copy in sums:
        copy.wait_recv()
    lse = log_sums(1)
    for d in range(1, NX):
        weights(1, 3 + d, lse[d])
    passed_on = [*on_up.values(), *on_down.values()]
    for copy in passed_on:
        copy.wait_send()
    def share_z(n):
        return remote(tfwd.at[:, part(n, 256)], gz_in.at[n], gzs.at[n], gzr.at[n], z_back)

    @pl.loop(0, 4)
    def _(n):
        to_s, to_z = adjacent_shares(1, n, part(n, 256))
        tfwd[:, part(n, 256)] = (gacc[1, n] + to_z).astype(BF16)
        gacc[0, n] = gacc[0, n] + to_s
        share_z(n).start()

    shares_z = [share_z(n) for n in range(4)]
    started.extend(shares_z)
    for d in range(1, NX):
        weights(1, d, lse[d])
    paired_weights(1, lse[0])
    products(1)

    def term_rows(which, n, i):
        rows = pl.ds(pl.multiple_of(which * 640 + i * 320, 64), 320)
        cols = part(n, 256)
        return (
            dot(h[rows, 0:512], txt[:, cols])
            + dot(h[rows, 512:1024], tadj[0, :, cols])
            + dot(h[rows, 1024:1536], tadj[1, :, cols])
        )

    def spot(n, p):
        return pl.ds(pl.multiple_of(n * 640 + p * 80, 16), 80)

    def pair_copy(n):
        return remote(core_out.at[n], core_in.at[n], cs.at[n], cr.at[n], sibling)

    def beside(k, d):
        return lax.rem((x, y)[k] + d, NX) + 4 * k

    def first_copy(n, k, d):
        return remote(
            piece.at[n, beside(k, d)], in1.at[n, k, d - 1],
            p1s.at[n, k, d - 1], p1r.at[n, k, d - 1], (x_peer, y_peer)[k](d),
        )

    first_y, second_y = {}, {}
    sides = [(pl.ds(0, HALF), up), (pl.ds(HALF, HALF), down)]

    def pass_share(n):
        shares_z[n].wait_recv()
        cols = slice(n * 256, (n + 1) * 256)
        aud[0, :, cols] = (gacc[0, n] + gz_in[n].astype(F32)).astype(BF16)
        for k, (rows, peer) in enumerate(sides):
            first_y[n, k] = send(aud.at[0, rows, cols], gfwd.at[n, rows], gys.at[0, k, n], gyr.at[0, k, n], peer)

    def forward_share(n):
        for k, (rows, peer) in enumerate(sides):
            first_y[n, k].wait_recv()
            second_y[n, k] = send(gfwd.at[n, rows], g_in.at[n, rows], gys.at[1, k, n], gyr.at[1, k, n], peer)

    @pl.loop(0, 5)
    def _(n):
        @pl.when(n < 4)
        def _():
            @pl.loop(0, 2)
            def _(i):
                core_out[n, part(i, 320), :] = term_rows(1 - c, n, i).astype(BF16)

            pair_copy(n).start()

            @pl.loop(0, 2)
            def _(i):
                sco[0, pl.ds(pl.multiple_of(n * 640 + i * 320, 64), 320), :] = term_rows(c, n, i)

        @pl.when(n > 0)
        def _():
            pair_copy(n - 1).wait_recv()

            @pl.loop(0, 8)
            def _(p):
                v = sco[0, spot(n - 1, p), :] + core_in[n - 1, pl.ds(pl.multiple_of(p * 80, 16), 80), :].astype(F32)
                sco[0, spot(n - 1, p), :] = v
                piece[n - 1, p] = v.astype(BF16)

            for d in range(1, NX):
                for k in range(2):
                    first_copy(n - 1, k, d).start()

    firsts = [first_copy(n, k, d) for n in range(4) for k in range(2) for d in range(1, NX)]
    started.extend(firsts)
    started.extend(pair_copy(n) for n in range(4))
    pass_share(0)

    @pl.loop(0, 4)
    def _(n):
        gown[n] = gown[n] + own_share(1, part(n, 256))

    for copy in firsts:
        copy.wait_recv()
    mine = (x, 4 + y)
    for n in range(4):
        for k in range(2):
            v = sco[0, spot(n, mine[k]), :]
            for d in range(3):
                v = v + in1[n, k, d].astype(F32)
            sum2[k, n] = v
            out2[k, n] = v.astype(BF16)
    seconds = []
    for d in range(1, NX):
        xd, yd = lax.rem(x + d, NX), lax.rem(y + d, NY)
        seconds.append(send(out2.at[0, yd], in2.at[0, d - 1], p2s.at[0, d - 1], p2r.at[0, d - 1], y_peer(d)))
        seconds.append(send(out2.at[1, xd], in2.at[1, d - 1], p2s.at[1, d - 1], p2r.at[1, d - 1], x_peer(d)))
    pass_share(1)

    for copy in seconds:
        copy.wait_recv()
    theirs = (y, x)
    tiles = [(k, i, j) for k in range(2) for i in range(5) for j in range(2)]
    for k in range(2):
        v = sum2[k, theirs[k]]
        for d in range(3):
            v = v + in2[k, d].astype(F32)
        for t, (k_, i, j) in enumerate(tiles):
            if k_ == k:
                tile = v[i * 16:(i + 1) * 16, j * 128:(j + 1) * 128]
                zown[t // 3, t % 3] = tile
                zb[t // 3, t % 3] = tile.astype(BF16)
    for t in range(20, 24):
        zown[t // 3, t % 3] = jnp.zeros((16, 128), F32)
        zb[t // 3, t % 3] = jnp.zeros((16, 128), BF16)
    thirds = []
    for d in range(1, NZ):
        zd = lax.rem(z + d, NZ)
        thirds.append(send(zb.at[zd], zin.at[d - 1], z1s.at[d - 1], z1r.at[d - 1], z_peer(d)))
    forward_share(0)
    pass_share(2)
    for copy in thirds:
        copy.wait_recv()
    v = zown[z]
    for d in range(NZ - 1):
        v = v + zin[d].astype(F32)
    zall[z] = (v * (SCALE / 256.0)).astype(BF16)
    fourths = [send(zall.at[z], zall.at[z], z2s.at[d - 1], z2r.at[d - 1], z_peer(d)) for d in range(1, NZ)]
    forward_share(1)
    for copy in fourths:
        copy.wait_recv()

    def block(p, rows=80, more=0):
        return pl.ds(pl.multiple_of(c * 640 + p * 80 + more, 16), rows)

    def columns(n, size=256, more=0):
        return pl.ds(pl.multiple_of(n * 256 + more, 128), size)

    for t, (k, i, j) in enumerate(tiles):
        pg_ref[block(mine[k], 16, 16 * i), columns(theirs[k], 128, 128 * j)] = zall[t // 3, t % 3]
    fifths = []
    for k in range(2):
        own = pg_ref.at[block(mine[k]), columns(theirs[k])]
        for d in range(1, NX):
            fifths.append(send(own, own, a2s.at[k, d - 1], a2r.at[k, d - 1], (y_peer, x_peer)[k](d)))
    pass_share(3)
    forward_share(2)
    for copy in fifths:
        copy.wait_recv()
    sixths, lasts = {}, []

    def to_sibling(p, k):
        rows = pg_ref.at[block(p)]
        lasts.append(send(rows, rows, ks.at[k], kr.at[k], sibling))

    low, high = pl.ds(0, 512), pl.ds(512, 512)

    def spread(k, i, p, cols, peer):
        rows = pg_ref.at[block(p), cols]
        sixths[k, i] = send(rows, rows, a1s.at[k, i], a1r.at[k, i], peer)

    ends = [(x_peer(1), x_peer(3)), (y_peer(1), y_peer(3))]
    for k in range(2):
        spread(k, 0, mine[k], low, ends[k][0])
        spread(k, 1, mine[k], high, ends[k][1])
    for k in range(2):
        spread(k, 2, mine[k], high, ends[k][0])
        spread(k, 3, mine[k], low, ends[k][1])
        to_sibling(mine[k], 4 * k)
    for k in range(2):
        sixths[k, 0].wait_recv()
        spread(k, 4, beside(k, 3), low, ends[k][0])
        sixths[k, 1].wait_recv()
        spread(k, 5, beside(k, 1), high, ends[k][1])
    forward_share(3)

    for n in range(4):
        for k in range(2):
            second_y[n, k].wait_recv()
        tgrad_ref[:, n * 256:(n + 1) * 256] = (SCALE * (gown[n] + g_in[n].astype(F32))).astype(BF16)

    for d, i, j in ((3, 0, 2), (1, 1, 3), (2, 4, 5)):
        for k in range(2):
            if d == 2:
                sixths[k, i].wait_recv()
            sixths[k, j].wait_recv()
            to_sibling(beside(k, d), 4 * k + d)
    for copy in lasts:
        copy.wait_recv()
    for copy in started:
        if not any(copy is other for other in passed_on):
            copy.wait_send()


def finish(loss_in, text_in, proj_in, loss_ref, text_ref, proj_ref):
    loss_ref[...] = loss_in[0, :]
    text_ref[...] = text_in[...]
    proj_ref[...] = proj_in[...].astype(F32)


def on_device(audio_emb, text_emb, proj_weight, pair_index):
    dma = pltpu.SemaphoreType.DMA
    hbm = pl.BlockSpec(memory_space=pl.ANY)
    vmem = pl.BlockSpec(memory_space=pltpu.VMEM)
    sems = []
    for shape in ((2, 6), (2, R // TR), (R // TR,), (2, 3), (4,), (2, 2, 4), (4,), (4, 2, 3), (2, 3), (7,), (7,), (2, 3), (2, 6), (8,)):
        sems += [dma(shape), dma(shape)]
    loss, text_grad, shares = pl.pallas_call(
        kernel,
        out_shape=(
            jax.ShapeDtypeStruct((1, R), F32),
            jax.ShapeDtypeStruct((R, E), BF16),
            jax.ShapeDtypeStruct((A, E), BF16),
        ),
        in_specs=[hbm, hbm, hbm, vmem],
        out_specs=(vmem, vmem, vmem),
        scratch_shapes=[
            pltpu.VMEM((4, R, A), BF16),
            pltpu.VMEM((4, A, R), BF16),
            pltpu.VMEM((A, E), BF16),
            pltpu.VMEM((R, E), BF16),
            pltpu.VMEM((2, R, E), BF16),
            pltpu.VMEM((R, E), BF16),
            pltpu.VMEM((4, R, E), BF16),
            pltpu.VMEM((2, 7 * R, HALF), F32),
            pltpu.VMEM((7, R, HALF), BF16),
            pltpu.VMEM((2, 7, 1, HALF), F32),
            pltpu.VMEM((2, 7, 1, HALF), F32),
            pltpu.VMEM((2, 8, HALF), F32),
            pltpu.VMEM((2, 3, 8, HALF), F32),
            pltpu.VMEM((A, 3 * R), F32),
            pltpu.VMEM((A, 3 * R), BF16),
            pltpu.VMEM((4, R, 256), BF16),
            pltpu.VMEM((2, 4, R, 256), F32),
            pltpu.VMEM((4, R, 256), F32),
            pltpu.VMEM((4, R, 256), BF16),
            pltpu.VMEM((4, R, 256), BF16),
            pltpu.VMEM((4, 640, 256), BF16),
            pltpu.VMEM((4, 640, 256), BF16),
            pltpu.VMEM((4, 8, 80, 256), BF16),
            pltpu.VMEM((4, 2, 3, 80, 256), BF16),
            pltpu.VMEM((2, 4, 80, 256), F32),
            pltpu.VMEM((2, 4, 80, 256), BF16),
            pltpu.VMEM((2, 3, 80, 256), BF16),
            pltpu.VMEM((8, 3, 16, 128), F32),
            pltpu.VMEM((8, 3, 16, 128), BF16),
            pltpu.VMEM((7, 3, 16, 128), BF16),
            pltpu.VMEM((8, 3, 16, 128), BF16),
            dma((3,)),
            *sems,
        ],
        compiler_params=pltpu.CompilerParams(
            collective_id=0, has_side_effects=True, vmem_limit_bytes=63 * 1024 * 1024
        ),
        cost_estimate=pl.CostEstimate(flops=24 * 10**9, bytes_accessed=16 * 2**20, transcendentals=4 * 2**20),
    )(audio_emb, text_emb, proj_weight, pair_index)
    return pl.pallas_call(
        finish,
        grid=(4,),
        out_shape=(
            jax.ShapeDtypeStruct((R,), F32),
            jax.ShapeDtypeStruct((R, E), BF16),
            jax.ShapeDtypeStruct((A, E), F32),
        ),
        in_specs=[
            pl.BlockSpec((1, R), lambda i: (0, 0)),
            pl.BlockSpec((R // 4, E), lambda i: (i, 0)),
            pl.BlockSpec((A // 4, E), lambda i: (i, 0)),
        ],
        out_specs=(
            pl.BlockSpec((R,), lambda i: (0,)),
            pl.BlockSpec((R // 4, E), lambda i: (i, 0)),
            pl.BlockSpec((A // 4, E), lambda i: (i, 0)),
        ),
        cost_estimate=pl.CostEstimate(flops=0, bytes_accessed=10 * 2**20, transcendentals=0),
    )(loss, text_grad, shares)


def solution(mesh):
    return jax.shard_map(
        on_device,
        mesh=mesh,
        in_specs=(P(("blk", "rep"), None), P(("blk", "rep"), None), P(), P(("blk", "rep"), None)),
        out_specs=(P(("blk", "rep")), P(("blk", "rep"), None), P()),
        check_vma=False,
    )
```

```python
import math

import jax
import jax.numpy as jnp
from jax import lax
from jax.experimental import pallas as pl
from jax.experimental.pallas import tpu as pltpu
from jax.sharding import PartitionSpec as P

A = 1280
E = 1024
R = 512
SCALE = 4.0 / math.sqrt(E)
NX, NY, NZ = 4, 4, 8
XR = 128
TR = 64
HALF = 256
NT = (((1,), (1,)), ((), ()))
F32 = jnp.float32
BF16 = jnp.bfloat16


def dot(a, b):
    return jnp.dot(a, b, preferred_element_type=F32)


def dot_nt(a, b):
    return lax.dot_general(a, b, NT, preferred_element_type=F32)


def part(i, size):
    return pl.ds(pl.multiple_of(i * size, size), size)


def kernel(
    aud_hbm, txt_hbm, w_hbm, pair_ref,
    loss_ref, tgrad_out, pg_out,
    aud, audt, w, txt, tadj, tfwd, tz, proj, sco, wt, wo, tops, totals, stat, stat_in,
    tgrad_ref, pg_ref, hacc, h, gz_in, gacc, gfwd, g_in,
    core_out, core_in, piece, in1, sum2, out2, in2, zown, zb, zin, zall,
    loc_sem, out_sem, xs, xr, ys, yr, es, er, zs, zr, ss, sr, gzs, gzr, gys, gyr,
    cs, cr, p1s, p1r, p2s, p2r, z1s, z1r, z2s, z2r, a2s, a2r, a1s, a1r, ks, kr,
):
    b = lax.axis_index("blk")
    rep = lax.axis_index("rep")
    x = lax.rem(b, NX)
    yh = lax.rem(lax.div(b, NX), 2)
    z = lax.div(b, NX * 2)
    c = lax.rem(rep, 2)
    y = yh * 2 + lax.div(rep, 2)

    def at(x_, y_, z_, c_):
        return ((z_ * 2 + lax.div(y_, 2)) * NX + x_, lax.rem(y_, 2) * 2 + c_)

    def x_peer(d):
        return at(lax.rem(x + d, NX), y, z, c)

    def y_peer(d):
        return at(x, lax.rem(y + d, NY), z, c)

    def z_peer(d):
        return at(x, y, lax.rem(z + d, NZ), c)

    sibling = at(x, y, z, 1 - c)
    step = 1 - 2 * yh
    z_next = at(x, y, lax.rem(z + step + NZ, NZ), c)
    z_back = at(x, y, lax.rem(z - step + NZ, NZ), c)

    started = []

    def remote(src, dst, s, r, device):
        return pltpu.make_async_remote_copy(
            src_ref=src, dst_ref=dst, send_sem=s, recv_sem=r,
            device_id=device, device_id_type=pl.DeviceIdType.MESH,
        )

    def send(src, dst, s, r, device):
        copy = remote(src, dst, s, r, device)
        copy.start()
        started.append(copy)
        return copy

    loads = [
        pltpu.make_async_copy(w_hbm, w, loc_sem.at[0]),
        pltpu.make_async_copy(aud_hbm, aud.at[0], loc_sem.at[1]),
        pltpu.make_async_copy(txt_hbm, txt, loc_sem.at[2]),
    ]
    for load in loads:
        load.start()

    barrier = pltpu.get_barrier_semaphore()
    peers = [x_peer(d) for d in range(1, NX)] + [y_peer(d) for d in range(1, NY)]
    peers += [z_peer(d) for d in range(1, NZ)] + [sibling]
    for peer in peers:
        pl.semaphore_signal(barrier, inc=1, device_id=peer, device_id_type=pl.DeviceIdType.MESH)
    pl.semaphore_wait(barrier, len(peers))

    right, left = x_peer(1), x_peer(3)
    up, down = y_peer(1), y_peer(3)
    rows_x = [pl.ds(i * XR, XR) for i in range(R // XR)]
    rows_t = [pl.ds(i * TR, TR) for i in range(R // TR)]
    n_up = R // TR // 2
    to_right, to_left, on_right, on_left = {}, {}, {}, {}
    to_up, to_down, on_up, on_down, on_z = {}, {}, {}, {}, {}

    def audio_out(half):
        i, j = 2 * half, 2 * half + 1
        for p, q in ((i, j), (j, i)):
            to_right[p] = send(aud_hbm.at[rows_x[p]], aud.at[1, rows_x[p]], xs.at[0, p], xr.at[0, p], right)
            to_left[q] = send(aud_hbm.at[rows_x[q]], aud.at[3, rows_x[q]], xs.at[1, q], xr.at[1, q], left)

    def audio_on(half):
        i, j = 2 * half, 2 * half + 1
        to_right[i].wait_recv()
        on_right[i] = send(aud.at[1, rows_x[i]], aud.at[2, rows_x[i]], xs.at[0, 4 + half], xr.at[0, 4 + half], right)
        to_left[j].wait_recv()
        on_left[j] = send(aud.at[3, rows_x[j]], aud.at[2, rows_x[j]], xs.at[1, 4 + half], xr.at[1, 4 + half], left)

    def text_out(i):
        k = n_up + i
        to_up[i] = send(txt_hbm.at[rows_t[i]], tfwd.at[rows_t[i]], ys.at[0, i], yr.at[0, i], up)
        to_down[k] = send(txt_hbm.at[rows_t[k]], tfwd.at[rows_t[k]], ys.at[0, k], yr.at[0, k], down)

    def text_on(i):
        k = n_up + i
        to_up[i].wait_recv()
        on_up[i] = send(tfwd.at[rows_t[i]], tadj.at[0, rows_t[i]], ys.at[1, i], yr.at[1, i], up)
        to_down[k].wait_recv()
        on_down[k] = send(tfwd.at[rows_t[k]], tadj.at[0, rows_t[k]], ys.at[1, k], yr.at[1, k], down)

    def text_z(i):
        k = n_up + i
        on_up[i].wait_recv()
        on_z[i] = send(tadj.at[0, rows_t[i]], tadj.at[1, rows_t[i]], zs.at[i], zr.at[i], z_next)
        on_down[k].wait_recv()
        on_z[k] = send(tadj.at[0, rows_t[k]], tadj.at[1, rows_t[k]], zs.at[k], zr.at[k], z_next)

    z_up, z_down = n_up - 1, 2 * n_up - 1
    ways = [(z_up, up), (z_down, down)]
    early, early_on, early_last = {}, {}, {}

    def early_out():
        for k, (i, _) in enumerate(ways):
            early[k] = send(txt_hbm.at[rows_t[i]], tz.at[0, k], es.at[0, k], er.at[0, k], z_back)

    def early_y():
        for k, (i, peer) in enumerate(ways):
            early[k].wait_recv()
            early_on[k] = send(tz.at[0, k], tz.at[1, k], es.at[1, k], er.at[1, k], peer)

    def early_end():
        for k, (i, peer) in enumerate(ways):
            early_on[k].wait_recv()
            early_last[k] = send(tz.at[1, k], tadj.at[1, rows_t[i]], es.at[2, k], er.at[2, k], peer)

    halves = [slice(0, HALF), slice(HALF, R)]

    def half(s):
        return part(s, HALF)

    def project(d, s):
        @pl.loop(0, 2)
        def _(n):
            cols = part(n, 512)
            proj[d, half(s), cols] = dot(aud[d, half(s), :], w[:, cols]).astype(BF16)

    def turn(d, s):
        @pl.loop(0, A // 128)
        def _(n):
            cols = part(n, 128)
            audt[d, cols, half(s)] = aud[d, half(s), cols].T

    def scores(s, index, text, d):
        @pl.loop(0, 2)
        def _(n):
            rows = pl.ds(pl.multiple_of(index * R + n * 256, 256), 256)
            sco[s, rows, :] = SCALE * dot_nt(text[part(n, 256), :], proj[d, half(s), :])

    def score_rows(index, n):
        return pl.ds(pl.multiple_of(index * R + n * 64, 64), 64)

    def exponents(s, index):
        def top_of(n, m):
            return jnp.maximum(m, jnp.max(sco[s, score_rows(index, n), :], axis=0, keepdims=True))

        m = lax.fori_loop(0, 8, top_of, jnp.full((1, HALF), -jnp.inf, F32))

        def total_of(n, t):
            e = jnp.exp(sco[s, score_rows(index, n), :] - m)
            sco[s, score_rows(index, n), :] = e
            return t + jnp.sum(e, axis=0, keepdims=True)

        tops[s, index] = m
        totals[s, index] = lax.fori_loop(0, 8, total_of, jnp.zeros((1, HALF), F32))

    def row_sums(s, d):
        m, t = tops[s, d], totals[s, d]
        if d > 0:
            m = jnp.maximum(m, tops[s, 3 + d])
            t = t * jnp.exp(tops[s, d] - m) + totals[s, 3 + d] * jnp.exp(tops[s, 3 + d] - m)
        stat[s, d:d + 1, :] = m
        stat[s, 4 + d:5 + d, :] = t

    def pair_scores(s):
        def block(n, paired):
            column = lax.broadcasted_iota(jnp.int32, (64, HALF), 0) + n * 64
            hot = (pair_ref[:, half(s)] == column).astype(F32)
            return paired + jnp.sum(sco[s, score_rows(0, n), :] * hot, axis=0, keepdims=True)

        loss_ref[:, half(s)] = lax.fori_loop(0, 8, block, jnp.zeros((1, HALF), F32))

    def sums_out(s):
        return [
            send(stat.at[s], stat_in.at[s, d - 1], ss.at[s, d - 1], sr.at[s, d - 1], x_peer(d))
            for d in range(1, NX)
        ]

    def log_sums(s):
        lse = []
        for d in range(NX):
            ms = [stat[s, d:d + 1, :]]
            ts = [stat[s, 4 + d:5 + d, :]]
            for back in range(1, NX):
                k = (d - back) % NX
                ms.append(stat_in[s, back - 1, k:k + 1, :])
                ts.append(stat_in[s, back - 1, 4 + k:5 + k, :])
            top = jnp.maximum(jnp.maximum(ms[0], ms[1]), jnp.maximum(ms[2], ms[3]))
            total = sum(t * jnp.exp(m - top) for m, t in zip(ms, ts))
            lse.append(top + jnp.log(total))
        return lse

    def weights(s, index, lse):
        factor = jnp.exp(tops[s, index] - lse)
        place = wt.at[index - 4] if index > 3 else wo.at[s, index]

        @pl.loop(0, 8)
        def _(n):
            place[part(n, 64), :] = (sco[s, score_rows(index, n), :] * factor).astype(BF16)

    def paired_weights(s, lse):
        factor = jnp.exp(tops[s, 0] - lse)

        @pl.loop(0, 8)
        def _(n):
            column = lax.broadcasted_iota(jnp.int32, (64, HALF), 0) + n * 64
            hot = (pair_ref[:, halves[s]] == column).astype(F32)
            wo[s, 0, part(n, 64), :] = (sco[s, score_rows(0, n), :] * factor - hot).astype(BF16)

        loss_ref[:, halves[s]] = lse - loss_ref[:, halves[s]]

    def via_z(d):
        return jnp.where(x >= d, 1 - yh, yh)

    zf = [None] + [via_z(d).astype(F32) for d in range(1, NX)]

    def adjacent_shares(s, n, cols):
        to_s, to_z = None, None
        for d in range(1, NX):
            g = dot(wt[d - 1], proj[d, halves[s], cols])
            gz = zf[d] * g
            to_z = gz if to_z is None else to_z + gz
            to_s = g - gz if to_s is None else to_s + (g - gz)
        return to_s, to_z

    def own_share(cols):
        g = None
        for s in range(2):
            for d in range(NX):
                v = dot(wo[s, d], proj[d, halves[s], cols])
                g = v if g is None else g + v
        return g

    def products(s):
        @pl.loop(0, 4)
        def _(n):
            rows = part(lax.div(n, 2), 640)
            j = lax.rem(n, 2)
            texts = part(j, 256)

            def keep(k, v):
                cols = part(2 * k + j, 256)
                if s == 0:
                    hacc[rows, cols] = v
                else:
                    h[rows, cols] = (hacc[rows, cols] + v).astype(BF16)

            own = dot_nt(audt[0, rows, halves[s]], wo[s, 0, texts, :])
            for d in range(1, NX):
                own = own + dot_nt(audt[d, rows, halves[s]], wo[s, d, texts, :])
            keep(0, own)
            to_s, to_z = None, None
            for d in range(1, NX):
                v = dot_nt(audt[d, rows, halves[s]], wt[d - 1, texts, :])
                vz = zf[d] * v
                to_z = vz if to_z is None else to_z + vz
                to_s = v - vz if to_s is None else to_s + (v - vz)
            keep(1, to_s)
            keep(2, to_z)

    def own_scores(s, d):
        scores(s, d, txt, d)
        exponents(s, d)
        turn(d, s)

    def adjacent_scores(s, d):
        scores(s, 3 + d, tadj.at[via_z(d)], d)
        exponents(s, 3 + d)

    audio_out(0)
    text_out(0)
    early_out()
    text_out(1)
    loads[0].wait()
    loads[1].wait()
    loads[2].wait()

    @pl.loop(0, 2)
    def _(s):
        project(0, s)
        scores(s, 0, txt, 0)
        pair_scores(s)
        exponents(s, 0)
        turn(0, s)

    text_on(0)
    text_out(2)
    text_on(1)
    early_y()
    text_out(3)
    audio_on(0)
    audio_out(1)
    row_sums(0, 0)
    row_sums(1, 0)
    text_z(0)
    text_on(2)
    text_z(1)
    early_end()
    text_on(3)
    to_right[1].wait_recv()
    to_left[0].wait_recv()

    @pl.loop(0, 2)
    def _(n):
        project(2 * n + 1, 0)
        own_scores(0, 2 * n + 1)

    text_z(2)
    on_right[0].wait_recv()
    on_left[1].wait_recv()
    project(2, 0)
    own_scores(0, 2)
    audio_on(1)
    for copy in [*on_z.values(), *early_last.values(), on_up[n_up - 1], on_down[2 * n_up - 1]]:
        copy.wait_recv()

    @pl.loop(1, 4)
    def _(d):
        adjacent_scores(0, d)

    for d in range(1, NX):
        row_sums(0, d)
    sums = sums_out(0)
    to_right[3].wait_recv()
    to_left[2].wait_recv()

    @pl.loop(0, 2)
    def _(n):
        d = 2 * n + 1
        project(d, 1)
        own_scores(1, d)
        adjacent_scores(1, d)

    for copy in sums:
        copy.wait_recv()
    lse = log_sums(0)
    for d in range(1, NX):
        weights(0, 3 + d, lse[d])
        weights(0, d, lse[d])
    paired_weights(0, lse[0])

    @pl.loop(0, 4)
    def _(n):
        to_s, to_z = adjacent_shares(0, n, part(n, 256))
        gacc[0, n] = to_s
        gacc[1, n] = to_z

    on_right[2].wait_recv()
    on_left[3].wait_recv()
    project(2, 1)
    scores(1, 2, txt, 2)
    exponents(1, 2)
    adjacent_scores(1, 2)
    for d in range(1, NX):
        row_sums(1, d)
    sums = sums_out(1)
    products(0)
    turn(2, 1)
    for copy in sums:
        copy.wait_recv()
    lse = log_sums(1)
    for d in range(1, NX):
        weights(1, 3 + d, lse[d])
    passed_on = [*on_up.values(), *on_down.values()]
    for copy in passed_on:
        copy.wait_send()
    def share_z(n):
        return remote(tfwd.at[:, part(n, 256)], gz_in.at[n], gzs.at[n], gzr.at[n], z_back)

    @pl.loop(0, 4)
    def _(n):
        to_s, to_z = adjacent_shares(1, n, part(n, 256))
        tfwd[:, part(n, 256)] = (gacc[1, n] + to_z).astype(BF16)
        gacc[0, n] = gacc[0, n] + to_s
        share_z(n).start()

    shares_z = [share_z(n) for n in range(4)]
    started.extend(shares_z)
    for d in range(1, NX):
        weights(1, d, lse[d])
    paired_weights(1, lse[0])
    products(1)

    def term_rows(which, n):
        rows = part(which, 640)
        cols = part(n, 256)
        return (
            dot(h[rows, 0:512], txt[:, cols])
            + dot(h[rows, 512:1024], tadj[0, :, cols])
            + dot(h[rows, 1024:1536], tadj[1, :, cols])
        )

    def spot(n, p):
        return pl.ds(pl.multiple_of(n * 640 + p * 80, 16), 80)

    def pair_copy(n):
        return remote(core_out.at[n], core_in.at[n], cs.at[n], cr.at[n], sibling)

    def beside(k, d):
        return lax.rem((x, y)[k] + d, NX) + 4 * k

    def first_copy(n, k, d):
        return remote(
            piece.at[n, beside(k, d)], in1.at[n, k, d - 1],
            p1s.at[n, k, d - 1], p1r.at[n, k, d - 1], (x_peer, y_peer)[k](d),
        )

    first_y, second_y = {}, {}
    sides = [(pl.ds(0, HALF), up), (pl.ds(HALF, HALF), down)]

    def pass_share(n):
        shares_z[n].wait_recv()
        cols = slice(n * 256, (n + 1) * 256)
        aud[0, :, cols] = (gacc[0, n] + gz_in[n].astype(F32)).astype(BF16)
        for k, (rows, peer) in enumerate(sides):
            first_y[n, k] = send(aud.at[0, rows, cols], gfwd.at[n, rows], gys.at[0, k, n], gyr.at[0, k, n], peer)

    def forward_share(n):
        for k, (rows, peer) in enumerate(sides):
            first_y[n, k].wait_recv()
            second_y[n, k] = send(gfwd.at[n, rows], g_in.at[n, rows], gys.at[1, k, n], gyr.at[1, k, n], peer)

    @pl.loop(0, 5)
    def _(n):
        @pl.when(n < 4)
        def _():
            core_out[n] = term_rows(1 - c, n).astype(BF16)
            pair_copy(n).start()
            sco[0, part(n, 640), :] = term_rows(c, n)

        @pl.when(n > 0)
        def _():
            pair_copy(n - 1).wait_recv()

            @pl.loop(0, 8)
            def _(p):
                v = sco[0, spot(n - 1, p), :] + core_in[n - 1, pl.ds(pl.multiple_of(p * 80, 16), 80), :].astype(F32)
                sco[0, spot(n - 1, p), :] = v
                piece[n - 1, p] = v.astype(BF16)

            for d in (2, 1, 3):
                for k in range(2):
                    first_copy(n - 1, k, d).start()

    firsts = [first_copy(n, k, d) for n in range(4) for k in range(2) for d in range(1, NX)]
    started.extend(firsts)
    started.extend(pair_copy(n) for n in range(4))
    pass_share(0)

    def own_gradient(first, last):
        @pl.loop(first, last)
        def _(n):
            cols = part(n, 256)
            hacc[0:R, cols] = own_share(cols)

    own_gradient(0, 2)
    for copy in firsts:
        copy.wait_recv()
    mine = (x, 4 + y)
    for n in range(4):
        for k in range(2):
            v = sco[0, spot(n, mine[k]), :]
            for d in range(3):
                v = v + in1[n, k, d].astype(F32)
            sum2[k, n] = v
            out2[k, n] = v.astype(BF16)
    seconds = []
    for d in (2, 1, 3):
        xd, yd = lax.rem(x + d, NX), lax.rem(y + d, NY)
        seconds.append(send(out2.at[0, yd], in2.at[0, d - 1], p2s.at[0, d - 1], p2r.at[0, d - 1], y_peer(d)))
        seconds.append(send(out2.at[1, xd], in2.at[1, d - 1], p2s.at[1, d - 1], p2r.at[1, d - 1], x_peer(d)))
    pass_share(1)
    own_gradient(2, 4)
    for copy in seconds:
        copy.wait_recv()
    theirs = (y, x)
    tiles = [(k, i, j) for k in range(2) for i in range(5) for j in range(2)]
    for k in range(2):
        v = sum2[k, theirs[k]]
        for d in range(3):
            v = v + in2[k, d].astype(F32)
        for t, (k_, i, j) in enumerate(tiles):
            if k_ == k:
                tile = v[i * 16:(i + 1) * 16, j * 128:(j + 1) * 128]
                zown[t // 3, t % 3] = tile
                zb[t // 3, t % 3] = tile.astype(BF16)
    for t in range(20, 24):
        zown[t // 3, t % 3] = jnp.zeros((16, 128), F32)
        zb[t // 3, t % 3] = jnp.zeros((16, 128), BF16)
    thirds = []
    far_first = (4, 3, 5, 2, 6, 1, 7)
    for d in far_first:
        zd = lax.rem(z + d, NZ)
        thirds.append(send(zb.at[zd], zin.at[d - 1], z1s.at[d - 1], z1r.at[d - 1], z_peer(d)))
    forward_share(0)
    pass_share(2)
    for copy in thirds:
        copy.wait_recv()
    v = zown[z]
    for d in range(NZ - 1):
        v = v + zin[d].astype(F32)
    zall[z] = (v * (SCALE / 256.0)).astype(BF16)
    fourths = [send(zall.at[z], zall.at[z], z2s.at[d - 1], z2r.at[d - 1], z_peer(d)) for d in far_first]
    forward_share(1)
    for copy in fourths:
        copy.wait_recv()

    def block(p, rows=80, more=0):
        return pl.ds(pl.multiple_of(c * 640 + p * 80 + more, 16), rows)

    def columns(n, size=256, more=0):
        return pl.ds(pl.multiple_of(n * 256 + more, 128), size)

    for t, (k, i, j) in enumerate(tiles):
        pg_ref[block(mine[k], 16, 16 * i), columns(theirs[k], 128, 128 * j)] = zall[t // 3, t % 3]
    fifths = []
    for k in range(2):
        own = pg_ref.at[block(mine[k]), columns(theirs[k])]
        for d in (2, 1, 3):
            fifths.append(send(own, own, a2s.at[k, d - 1], a2r.at[k, d - 1], (y_peer, x_peer)[k](d)))
    pass_share(3)
    forward_share(2)
    for copy in fifths:
        copy.wait_recv()
    sixths, lasts, written, blocks = {}, [], [], []

    def write(src, dst, k):
        copy = pltpu.make_async_copy(src, dst, out_sem.at[k])
        copy.start()
        written.append(copy)

    def to_sibling(p, k):
        rows = pg_ref.at[block(p)]
        write(rows, pg_out.at[block(p)], k)
        blocks.append((p, k))
        lasts.append(send(rows, rows, ks.at[k], kr.at[k], sibling))

    low, high = pl.ds(0, 512), pl.ds(512, 512)

    def spread(k, i, p, cols, peer):
        rows = pg_ref.at[block(p), cols]
        sixths[k, i] = send(rows, rows, a1s.at[k, i], a1r.at[k, i], peer)

    ends = [(x_peer(1), x_peer(3)), (y_peer(1), y_peer(3))]
    for k in range(2):
        spread(k, 0, mine[k], low, ends[k][0])
        spread(k, 1, mine[k], high, ends[k][1])
    for k in range(2):
        spread(k, 2, mine[k], high, ends[k][0])
        spread(k, 3, mine[k], low, ends[k][1])
        to_sibling(mine[k], 4 * k)
    for k in range(2):
        sixths[k, 0].wait_recv()
        spread(k, 4, beside(k, 3), low, ends[k][0])
        sixths[k, 1].wait_recv()
        spread(k, 5, beside(k, 1), high, ends[k][1])
    forward_share(3)

    for n in range(4):
        for k in range(2):
            second_y[n, k].wait_recv()
        tgrad_ref[:, n * 256:(n + 1) * 256] = (SCALE * (hacc[0:R, n * 256:(n + 1) * 256] + g_in[n].astype(F32))).astype(BF16)
    write(tgrad_ref, tgrad_out, 16)

    for d, i, j in ((3, 0, 2), (1, 1, 3), (2, 4, 5)):
        for k in range(2):
            if d == 2:
                sixths[k, i].wait_recv()
            sixths[k, j].wait_recv()
            to_sibling(beside(k, d), 4 * k + d)
    for copy, (p, k) in zip(lasts, blocks):
        copy.wait_recv()
        rows = pl.ds(pl.multiple_of((1 - c) * 640 + p * 80, 16), 80)
        write(pg_ref.at[rows], pg_out.at[rows], 8 + k)
    for copy in written:
        copy.wait()
    for copy in started:
        if not any(copy is other for other in passed_on):
            copy.wait_send()


def finish(loss_in, text_in, proj_in, loss_ref, text_ref, proj_ref):
    loss_ref[...] = loss_in[0, :]
    text_ref[...] = text_in[...]
    proj_ref[...] = proj_in[...].astype(F32)


def on_device(audio_emb, text_emb, proj_weight, pair_index):
    dma = pltpu.SemaphoreType.DMA
    hbm = pl.BlockSpec(memory_space=pl.ANY)
    vmem = pl.BlockSpec(memory_space=pltpu.VMEM)
    sems = []
    for shape in ((2, 6), (2, R // TR), (3, 2), (R // TR,), (2, 3), (4,), (2, 2, 4), (4,), (4, 2, 3), (2, 3), (7,), (7,), (2, 3), (2, 6), (8,)):
        sems += [dma(shape), dma(shape)]
    loss, text_grad, shares = pl.pallas_call(
        kernel,
        out_shape=(
            jax.ShapeDtypeStruct((1, R), F32),
            jax.ShapeDtypeStruct((R, E), BF16),
            jax.ShapeDtypeStruct((A, E), BF16),
        ),
        in_specs=[hbm, hbm, hbm, vmem],
        out_specs=(vmem, hbm, hbm),
        scratch_shapes=[
            pltpu.VMEM((4, R, A), BF16),
            pltpu.VMEM((4, A, R), BF16),
            pltpu.VMEM((A, E), BF16),
            pltpu.VMEM((R, E), BF16),
            pltpu.VMEM((2, R, E), BF16),
            pltpu.VMEM((R, E), BF16),
            pltpu.VMEM((2, 2, TR, E), BF16),
            pltpu.VMEM((4, R, E), BF16),
            pltpu.VMEM((2, 7 * R, HALF), F32),
            pltpu.VMEM((3, R, HALF), BF16),
            pltpu.VMEM((2, 4, R, HALF), BF16),
            pltpu.VMEM((2, 7, 1, HALF), F32),
            pltpu.VMEM((2, 7, 1, HALF), F32),
            pltpu.VMEM((2, 8, HALF), F32),
            pltpu.VMEM((2, 3, 8, HALF), F32),
            pltpu.VMEM((R, E), BF16),
            pltpu.VMEM((A, E), BF16),
            pltpu.VMEM((A, 3 * R), F32),
            pltpu.VMEM((A, 3 * R), BF16),
            pltpu.VMEM((4, R, 256), BF16),
            pltpu.VMEM((2, 4, R, 256), F32),
            pltpu.VMEM((4, R, 256), BF16),
            pltpu.VMEM((4, R, 256), BF16),
            pltpu.VMEM((4, 640, 256), BF16),
            pltpu.VMEM((4, 640, 256), BF16),
            pltpu.VMEM((4, 8, 80, 256), BF16),
            pltpu.VMEM((4, 2, 3, 80, 256), BF16),
            pltpu.VMEM((2, 4, 80, 256), F32),
            pltpu.VMEM((2, 4, 80, 256), BF16),
            pltpu.VMEM((2, 3, 80, 256), BF16),
            pltpu.VMEM((8, 3, 16, 128), F32),
            pltpu.VMEM((8, 3, 16, 128), BF16),
            pltpu.VMEM((7, 3, 16, 128), BF16),
            pltpu.VMEM((8, 3, 16, 128), BF16),
            dma((3,)),
            dma((17,)),
            *sems,
        ],
        compiler_params=pltpu.CompilerParams(
            collective_id=0, has_side_effects=True, vmem_limit_bytes=63 * 1024 * 1024
        ),
        cost_estimate=pl.CostEstimate(flops=24 * 10**9, bytes_accessed=16 * 2**20, transcendentals=4 * 2**20),
    )(audio_emb, text_emb, proj_weight, pair_index)
    return pl.pallas_call(
        finish,
        grid=(2,),
        out_shape=(
            jax.ShapeDtypeStruct((R,), F32),
            jax.ShapeDtypeStruct((R, E), BF16),
            jax.ShapeDtypeStruct((A, E), F32),
        ),
        in_specs=[
            pl.BlockSpec((1, R), lambda i: (0, 0)),
            pl.BlockSpec((R // 2, E), lambda i: (i, 0)),
            pl.BlockSpec((A // 2, E), lambda i: (i, 0)),
        ],
        out_specs=(
            pl.BlockSpec((R,), lambda i: (0,)),
            pl.BlockSpec((R // 2, E), lambda i: (i, 0)),
            pl.BlockSpec((A // 2, E), lambda i: (i, 0)),
        ),
        cost_estimate=pl.CostEstimate(flops=0, bytes_accessed=10 * 2**20, transcendentals=0),
    )(loss, text_grad, shares)


def solution(mesh):
    return jax.shard_map(
        on_device,
        mesh=mesh,
        in_specs=(P(("blk", "rep"), None), P(("blk", "rep"), None), P(), P(("blk", "rep"), None)),
        out_specs=(P(("blk", "rep")), P(("blk", "rep"), None), P()),
        check_vma=False,
    )
```

```python
import math

import jax
import jax.numpy as jnp
from jax import lax
from jax.experimental import pallas as pl
from jax.experimental.pallas import tpu as pltpu
from jax.sharding import PartitionSpec as P

A = 1280
E = 1024
R = 512
SCALE = 4.0 / math.sqrt(E)
NX, NY, NZ = 4, 4, 8
XR = 128
TR = 64
HALF = 256
NT = (((1,), (1,)), ((), ()))
F32 = jnp.float32
BF16 = jnp.bfloat16


def dot(a, b):
    return jnp.dot(a, b, preferred_element_type=F32)


def dot_nt(a, b):
    return lax.dot_general(a, b, NT, preferred_element_type=F32)


def part(i, size):
    return pl.ds(pl.multiple_of(i * size, size), size)


def kernel(
    aud_hbm, txt_hbm, w_hbm, pair_ref,
    loss_ref, tgrad_out, pg_out,
    aud, audt, w, txt, tadj, tfwd, tz, proj, sco, wt, wo, tops, totals, stat, stat_in,
    tgrad_ref, pg_ref, hacc, h, gz_in, gacc, gfwd, g_in,
    core_out, core_in, piece, in1, sum2, out2, in2, zown, zb, zin, zall,
    loc_sem, out_sem, xs, xr, ys, yr, es, er, zs, zr, ss, sr, gzs, gzr, gys, gyr,
    cs, cr, p1s, p1r, p2s, p2r, z1s, z1r, z2s, z2r, a2s, a2r, a1s, a1r, ks, kr,
):
    b = lax.axis_index("blk")
    rep = lax.axis_index("rep")
    x = lax.rem(b, NX)
    yh = lax.rem(lax.div(b, NX), 2)
    z = lax.div(b, NX * 2)
    c = lax.rem(rep, 2)
    y = yh * 2 + lax.div(rep, 2)

    def at(x_, y_, z_, c_):
        return ((z_ * 2 + lax.div(y_, 2)) * NX + x_, lax.rem(y_, 2) * 2 + c_)

    def x_peer(d):
        return at(lax.rem(x + d, NX), y, z, c)

    def y_peer(d):
        return at(x, lax.rem(y + d, NY), z, c)

    def z_peer(d):
        return at(x, y, lax.rem(z + d, NZ), c)

    sibling = at(x, y, z, 1 - c)
    step = 1 - 2 * yh
    z_next = at(x, y, lax.rem(z + step + NZ, NZ), c)
    z_back = at(x, y, lax.rem(z - step + NZ, NZ), c)

    started = []

    def remote(src, dst, s, r, device):
        return pltpu.make_async_remote_copy(
            src_ref=src, dst_ref=dst, send_sem=s, recv_sem=r,
            device_id=device, device_id_type=pl.DeviceIdType.MESH,
        )

    def send(src, dst, s, r, device):
        copy = remote(src, dst, s, r, device)
        copy.start()
        started.append(copy)
        return copy

    loads = [
        pltpu.make_async_copy(w_hbm, w, loc_sem.at[0]),
        pltpu.make_async_copy(aud_hbm, aud.at[0], loc_sem.at[1]),
        pltpu.make_async_copy(txt_hbm, txt, loc_sem.at[2]),
    ]
    for load in loads:
        load.start()

    barrier = pltpu.get_barrier_semaphore()
    peers = [x_peer(d) for d in range(1, NX)] + [y_peer(d) for d in range(1, NY)]
    peers += [z_peer(d) for d in range(1, NZ)] + [sibling]
    for peer in peers:
        pl.semaphore_signal(barrier, inc=1, device_id=peer, device_id_type=pl.DeviceIdType.MESH)
    pl.semaphore_wait(barrier, len(peers))

    right, left = x_peer(1), x_peer(3)
    up, down = y_peer(1), y_peer(3)
    rows_x = [pl.ds(i * XR, XR) for i in range(R // XR)]
    rows_t = [pl.ds(i * TR, TR) for i in range(R // TR)]
    n_up = R // TR // 2
    to_right, to_left, on_right, on_left = {}, {}, {}, {}
    to_up, to_down, on_up, on_down, on_z = {}, {}, {}, {}, {}

    def audio_out(half):
        i, j = 2 * half, 2 * half + 1
        for p, q in ((i, j), (j, i)):
            to_right[p] = send(aud_hbm.at[rows_x[p]], aud.at[1, rows_x[p]], xs.at[0, p], xr.at[0, p], right)
            to_left[q] = send(aud_hbm.at[rows_x[q]], aud.at[3, rows_x[q]], xs.at[1, q], xr.at[1, q], left)

    def audio_on(half):
        i, j = 2 * half, 2 * half + 1
        to_right[i].wait_recv()
        on_right[i] = send(aud.at[1, rows_x[i]], aud.at[2, rows_x[i]], xs.at[0, 4 + half], xr.at[0, 4 + half], right)
        to_left[j].wait_recv()
        on_left[j] = send(aud.at[3, rows_x[j]], aud.at[2, rows_x[j]], xs.at[1, 4 + half], xr.at[1, 4 + half], left)

    def text_out(i):
        k = n_up + i
        to_up[i] = send(txt_hbm.at[rows_t[i]], tfwd.at[rows_t[i]], ys.at[0, i], yr.at[0, i], up)
        to_down[k] = send(txt_hbm.at[rows_t[k]], tfwd.at[rows_t[k]], ys.at[0, k], yr.at[0, k], down)

    def text_on(i):
        k = n_up + i
        to_up[i].wait_recv()
        on_up[i] = send(tfwd.at[rows_t[i]], tadj.at[0, rows_t[i]], ys.at[1, i], yr.at[1, i], up)
        to_down[k].wait_recv()
        on_down[k] = send(tfwd.at[rows_t[k]], tadj.at[0, rows_t[k]], ys.at[1, k], yr.at[1, k], down)

    def text_z(i):
        k = n_up + i
        on_up[i].wait_recv()
        on_z[i] = send(tadj.at[0, rows_t[i]], tadj.at[1, rows_t[i]], zs.at[i], zr.at[i], z_next)
        on_down[k].wait_recv()
        on_z[k] = send(tadj.at[0, rows_t[k]], tadj.at[1, rows_t[k]], zs.at[k], zr.at[k], z_next)

    z_up, z_down = n_up - 1, 2 * n_up - 1
    ways = [(z_up, up), (z_down, down)]
    early, early_on, early_last = {}, {}, {}

    def early_out():
        for k, (i, _) in enumerate(ways):
            early[k] = send(txt_hbm.at[rows_t[i]], tz.at[0, k], es.at[0, k], er.at[0, k], z_back)

    def early_y():
        for k, (i, peer) in enumerate(ways):
            early[k].wait_recv()
            early_on[k] = send(tz.at[0, k], tz.at[1, k], es.at[1, k], er.at[1, k], peer)

    def early_end():
        for k, (i, peer) in enumerate(ways):
            early_on[k].wait_recv()
            early_last[k] = send(tz.at[1, k], tadj.at[1, rows_t[i]], es.at[2, k], er.at[2, k], peer)

    halves = [slice(0, HALF), slice(HALF, R)]

    def half(s):
        return part(s, HALF)

    def project(d, s):
        @pl.loop(0, 2)
        def _(n):
            cols = part(n, 512)
            proj[d, half(s), cols] = dot(aud[d, half(s), :], w[:, cols]).astype(BF16)

    def turn(d, s):
        @pl.loop(0, A // 128)
        def _(n):
            cols = part(n, 128)
            audt[d, cols, half(s)] = aud[d, half(s), cols].T

    def scores(s, index, text, d):
        @pl.loop(0, 2)
        def _(n):
            rows = pl.ds(pl.multiple_of(index * R + n * 256, 256), 256)
            sco[s, rows, :] = SCALE * dot_nt(text[part(n, 256), :], proj[d, half(s), :])

    def score_rows(index, n):
        return pl.ds(pl.multiple_of(index * R + n * 64, 64), 64)

    def exponents(s, index):
        def top_of(n, m):
            return jnp.maximum(m, jnp.max(sco[s, score_rows(index, n), :], axis=0, keepdims=True))

        m = lax.fori_loop(0, 8, top_of, jnp.full((1, HALF), -jnp.inf, F32))

        def total_of(n, t):
            e = jnp.exp(sco[s, score_rows(index, n), :] - m)
            sco[s, score_rows(index, n), :] = e
            return t + jnp.sum(e, axis=0, keepdims=True)

        tops[s, index] = m
        totals[s, index] = lax.fori_loop(0, 8, total_of, jnp.zeros((1, HALF), F32))

    def row_sums(s, d):
        m, t = tops[s, d], totals[s, d]
        if d > 0:
            m = jnp.maximum(m, tops[s, 3 + d])
            t = t * jnp.exp(tops[s, d] - m) + totals[s, 3 + d] * jnp.exp(tops[s, 3 + d] - m)
        stat[s, d:d + 1, :] = m
        stat[s, 4 + d:5 + d, :] = t

    def pair_scores(s):
        def block(n, paired):
            column = lax.broadcasted_iota(jnp.int32, (64, HALF), 0) + n * 64
            hot = (pair_ref[:, half(s)] == column).astype(F32)
            return paired + jnp.sum(sco[s, score_rows(0, n), :] * hot, axis=0, keepdims=True)

        loss_ref[:, half(s)] = lax.fori_loop(0, 8, block, jnp.zeros((1, HALF), F32))

    def sums_out(s):
        return [
            send(stat.at[s], stat_in.at[s, d - 1], ss.at[s, d - 1], sr.at[s, d - 1], x_peer(d))
            for d in range(1, NX)
        ]

    def log_sums(s):
        lse = []
        for d in range(NX):
            ms = [stat[s, d:d + 1, :]]
            ts = [stat[s, 4 + d:5 + d, :]]
            for back in range(1, NX):
                k = (d - back) % NX
                ms.append(stat_in[s, back - 1, k:k + 1, :])
                ts.append(stat_in[s, back - 1, 4 + k:5 + k, :])
            top = jnp.maximum(jnp.maximum(ms[0], ms[1]), jnp.maximum(ms[2], ms[3]))
            total = sum(t * jnp.exp(m - top) for m, t in zip(ms, ts))
            lse.append(top + jnp.log(total))
        return lse

    def weights(s, index, lse):
        factor = jnp.exp(tops[s, index] - lse)
        place = wt.at[index - 4] if index > 3 else wo.at[s, index]

        @pl.loop(0, 8)
        def _(n):
            place[part(n, 64), :] = (sco[s, score_rows(index, n), :] * factor).astype(BF16)

    def paired_weights(s, lse):
        factor = jnp.exp(tops[s, 0] - lse)

        @pl.loop(0, 8)
        def _(n):
            column = lax.broadcasted_iota(jnp.int32, (64, HALF), 0) + n * 64
            hot = (pair_ref[:, halves[s]] == column).astype(F32)
            wo[s, 0, part(n, 64), :] = (sco[s, score_rows(0, n), :] * factor - hot).astype(BF16)

        loss_ref[:, halves[s]] = lse - loss_ref[:, halves[s]]

    def via_z(d):
        return jnp.where(x >= d, 1 - yh, yh)

    zf = [None] + [via_z(d).astype(F32) for d in range(1, NX)]

    def adjacent_shares(s, n, cols):
        to_s, to_z = None, None
        for d in range(1, NX):
            g = dot(wt[d - 1], proj[d, halves[s], cols])
            gz = zf[d] * g
            to_z = gz if to_z is None else to_z + gz
            to_s = g - gz if to_s is None else to_s + (g - gz)
        return to_s, to_z

    def own_share(cols):
        g = None
        for s in range(2):
            for d in range(NX):
                v = dot(wo[s, d], proj[d, halves[s], cols])
                g = v if g is None else g + v
        return g

    def products(s):
        @pl.loop(0, 4)
        def _(n):
            rows = part(lax.div(n, 2), 640)
            j = lax.rem(n, 2)
            texts = part(j, 256)

            def keep(k, v):
                cols = part(2 * k + j, 256)
                if s == 0:
                    hacc[rows, cols] = v
                else:
                    h[rows, cols] = (hacc[rows, cols] + v).astype(BF16)

            own = dot_nt(audt[0, rows, halves[s]], wo[s, 0, texts, :])
            for d in range(1, NX):
                own = own + dot_nt(audt[d, rows, halves[s]], wo[s, d, texts, :])
            keep(0, own)
            to_s, to_z = None, None
            for d in range(1, NX):
                v = dot_nt(audt[d, rows, halves[s]], wt[d - 1, texts, :])
                vz = zf[d] * v
                to_z = vz if to_z is None else to_z + vz
                to_s = v - vz if to_s is None else to_s + (v - vz)
            keep(1, to_s)
            keep(2, to_z)

    def own_scores(s, d):
        scores(s, d, txt, d)
        exponents(s, d)
        turn(d, s)

    def adjacent_scores(s, d):
        scores(s, 3 + d, tadj.at[via_z(d)], d)
        exponents(s, 3 + d)

    audio_out(0)
    text_out(0)
    early_out()
    text_out(1)
    loads[0].wait()
    loads[1].wait()
    loads[2].wait()

    @pl.loop(0, 2)
    def _(s):
        project(0, s)
        scores(s, 0, txt, 0)
        pair_scores(s)
        exponents(s, 0)
        turn(0, s)

    text_on(0)
    text_out(2)
    text_on(1)
    early_y()
    text_out(3)
    audio_on(0)
    audio_out(1)
    row_sums(0, 0)
    row_sums(1, 0)
    text_z(0)
    text_on(2)
    text_z(1)
    early_end()
    text_on(3)
    to_right[1].wait_recv()
    to_left[0].wait_recv()

    @pl.loop(0, 2)
    def _(n):
        project(2 * n + 1, 0)
        own_scores(0, 2 * n + 1)

    text_z(2)
    on_right[0].wait_recv()
    on_left[1].wait_recv()
    project(2, 0)
    own_scores(0, 2)
    audio_on(1)
    for copy in [*on_z.values(), *early_last.values(), on_up[n_up - 1], on_down[2 * n_up - 1]]:
        copy.wait_recv()

    @pl.loop(1, 4)
    def _(d):
        adjacent_scores(0, d)

    for d in range(1, NX):
        row_sums(0, d)
    sums = sums_out(0)
    to_right[3].wait_recv()
    to_left[2].wait_recv()

    @pl.loop(0, 2)
    def _(n):
        d = 2 * n + 1
        project(d, 1)
        own_scores(1, d)
        adjacent_scores(1, d)

    for copy in sums:
        copy.wait_recv()
    lse = log_sums(0)
    for d in range(1, NX):
        weights(0, 3 + d, lse[d])
        weights(0, d, lse[d])
    paired_weights(0, lse[0])

    @pl.loop(0, 4)
    def _(n):
        to_s, to_z = adjacent_shares(0, n, part(n, 256))
        gacc[0, n] = to_s
        gacc[1, n] = to_z

    on_right[2].wait_recv()
    on_left[3].wait_recv()
    project(2, 1)
    scores(1, 2, txt, 2)
    exponents(1, 2)
    adjacent_scores(1, 2)
    for d in range(1, NX):
        row_sums(1, d)
    sums = sums_out(1)
    products(0)
    turn(2, 1)
    for copy in sums:
        copy.wait_recv()
    lse = log_sums(1)
    for d in range(1, NX):
        weights(1, 3 + d, lse[d])
    passed_on = [*on_up.values(), *on_down.values()]
    for copy in passed_on:
        copy.wait_send()
    def share_z(n):
        return remote(tfwd.at[:, part(n, 256)], gz_in.at[n], gzs.at[n], gzr.at[n], z_back)

    def last_shares(first, last):
        @pl.loop(first, last)
        def _(n):
            to_s, to_z = adjacent_shares(1, n, part(n, 256))
            tfwd[:, part(n, 256)] = (gacc[1, n] + to_z).astype(BF16)
            gacc[0, n] = gacc[0, n] + to_s
            share_z(n).start()

    last_shares(0, 1)
    shares_z = [share_z(n) for n in range(4)]
    started.extend(shares_z)
    for d in range(1, NX):
        weights(1, d, lse[d])
    paired_weights(1, lse[0])
    products(1)
    last_shares(1, 2)

    def term_rows(which, n):
        rows = part(which, 640)
        cols = part(n, 256)
        return (
            dot(h[rows, 0:512], txt[:, cols])
            + dot(h[rows, 512:1024], tadj[0, :, cols])
            + dot(h[rows, 1024:1536], tadj[1, :, cols])
        )

    def spot(n, p):
        return pl.ds(pl.multiple_of(n * 640 + p * 80, 16), 80)

    def pair_copy(n):
        return remote(core_out.at[n], core_in.at[n], cs.at[n], cr.at[n], sibling)

    def beside(k, d):
        return lax.rem((x, y)[k] + d, NX) + 4 * k

    def first_copy(n, k, d):
        return remote(
            piece.at[n, beside(k, d)], in1.at[n, k, d - 1],
            p1s.at[n, k, d - 1], p1r.at[n, k, d - 1], (x_peer, y_peer)[k](d),
        )

    first_y, second_y = {}, {}
    sides = [(pl.ds(0, HALF), up), (pl.ds(HALF, HALF), down)]

    def pass_share(n):
        shares_z[n].wait_recv()
        cols = slice(n * 256, (n + 1) * 256)
        aud[0, :, cols] = (gacc[0, n] + gz_in[n].astype(F32)).astype(BF16)
        for k, (rows, peer) in enumerate(sides):
            first_y[n, k] = send(aud.at[0, rows, cols], gfwd.at[n, rows], gys.at[0, k, n], gyr.at[0, k, n], peer)

    def forward_share(n):
        for k, (rows, peer) in enumerate(sides):
            first_y[n, k].wait_recv()
            second_y[n, k] = send(gfwd.at[n, rows], g_in.at[n, rows], gys.at[1, k, n], gyr.at[1, k, n], peer)

    @pl.loop(0, 5)
    def _(n):
        @pl.when(n < 4)
        def _():
            core_out[n] = term_rows(1 - c, n).astype(BF16)
            pair_copy(n).start()
            sco[0, part(n, 640), :] = term_rows(c, n)

        @pl.when(n > 0)
        def _():
            pair_copy(n - 1).wait_recv()

            @pl.loop(0, 8)
            def _(p):
                v = sco[0, spot(n - 1, p), :] + core_in[n - 1, pl.ds(pl.multiple_of(p * 80, 16), 80), :].astype(F32)
                sco[0, spot(n - 1, p), :] = v
                piece[n - 1, p] = v.astype(BF16)

            for d in (2, 1, 3):
                for k in range(2):
                    first_copy(n - 1, k, d).start()

    firsts = [first_copy(n, k, d) for n in range(4) for k in range(2) for d in range(1, NX)]
    started.extend(firsts)
    started.extend(pair_copy(n) for n in range(4))
    last_shares(2, 4)
    pass_share(0)

    def own_gradient(first, last):
        @pl.loop(first, last)
        def _(n):
            cols = part(n, 256)
            hacc[0:R, cols] = own_share(cols)

    for copy in firsts:
        copy.wait_recv()
    mine = (x, 4 + y)
    for n in range(4):
        for k in range(2):
            v = sco[0, spot(n, mine[k]), :]
            for d in range(3):
                v = v + in1[n, k, d].astype(F32)
            sum2[k, n] = v
            out2[k, n] = v.astype(BF16)
    seconds = []
    for d in (2, 1, 3):
        xd, yd = lax.rem(x + d, NX), lax.rem(y + d, NY)
        seconds.append(send(out2.at[0, yd], in2.at[0, d - 1], p2s.at[0, d - 1], p2r.at[0, d - 1], y_peer(d)))
        seconds.append(send(out2.at[1, xd], in2.at[1, d - 1], p2s.at[1, d - 1], p2r.at[1, d - 1], x_peer(d)))
    pass_share(1)
    own_gradient(0, 1)
    for copy in seconds:
        copy.wait_recv()
    theirs = (y, x)
    tiles = [(k, i, j) for k in range(2) for i in range(5) for j in range(2)]
    for k in range(2):
        v = sum2[k, theirs[k]]
        for d in range(3):
            v = v + in2[k, d].astype(F32)
        for t, (k_, i, j) in enumerate(tiles):
            if k_ == k:
                tile = v[i * 16:(i + 1) * 16, j * 128:(j + 1) * 128]
                zown[t // 3, t % 3] = tile
                zb[t // 3, t % 3] = tile.astype(BF16)
    for t in range(20, 24):
        zown[t // 3, t % 3] = jnp.zeros((16, 128), F32)
        zb[t // 3, t % 3] = jnp.zeros((16, 128), BF16)
    thirds = []
    far_first = (4, 3, 5, 2, 6, 1, 7)
    for d in far_first:
        zd = lax.rem(z + d, NZ)
        thirds.append(send(zb.at[zd], zin.at[d - 1], z1s.at[d - 1], z1r.at[d - 1], z_peer(d)))
    forward_share(0)
    own_gradient(1, 3)
    for copy in thirds:
        copy.wait_recv()
    v = zown[z]
    for d in range(NZ - 1):
        v = v + zin[d].astype(F32)
    zall[z] = (v * (SCALE / 256.0)).astype(BF16)
    fourths = [send(zall.at[z], zall.at[z], z2s.at[d - 1], z2r.at[d - 1], z_peer(d)) for d in far_first]
    forward_share(1)
    pass_share(2)
    own_gradient(3, 4)
    for copy in fourths:
        copy.wait_recv()

    def block(p, rows=80, more=0):
        return pl.ds(pl.multiple_of(c * 640 + p * 80 + more, 16), rows)

    def columns(n, size=256, more=0):
        return pl.ds(pl.multiple_of(n * 256 + more, 128), size)

    for t, (k, i, j) in enumerate(tiles):
        pg_ref[block(mine[k], 16, 16 * i), columns(theirs[k], 128, 128 * j)] = zall[t // 3, t % 3]
    fifths = []
    for k in range(2):
        own = pg_ref.at[block(mine[k]), columns(theirs[k])]
        for d in (2, 1, 3):
            fifths.append(send(own, own, a2s.at[k, d - 1], a2r.at[k, d - 1], (y_peer, x_peer)[k](d)))
    pass_share(3)
    forward_share(2)
    for copy in fifths:
        copy.wait_recv()
    sixths, lasts, written, blocks = {}, [], [], []

    def write(src, dst, k):
        copy = pltpu.make_async_copy(src, dst, out_sem.at[k])
        copy.start()
        written.append(copy)

    def to_sibling(p, k):
        rows = pg_ref.at[block(p)]
        write(rows, pg_out.at[block(p)], k)
        blocks.append((p, k))
        lasts.append(send(rows, rows, ks.at[k], kr.at[k], sibling))

    low, high = pl.ds(0, 512), pl.ds(512, 512)

    def spread(k, i, p, cols, peer):
        rows = pg_ref.at[block(p), cols]
        sixths[k, i] = send(rows, rows, a1s.at[k, i], a1r.at[k, i], peer)

    ends = [(x_peer(1), x_peer(3)), (y_peer(1), y_peer(3))]
    for k in range(2):
        spread(k, 0, mine[k], low, ends[k][0])
        spread(k, 1, mine[k], high, ends[k][1])
    for k in range(2):
        spread(k, 2, mine[k], high, ends[k][0])
        spread(k, 3, mine[k], low, ends[k][1])
        to_sibling(mine[k], 4 * k)
    for k in range(2):
        sixths[k, 0].wait_recv()
        spread(k, 4, beside(k, 3), low, ends[k][0])
        sixths[k, 1].wait_recv()
        spread(k, 5, beside(k, 1), high, ends[k][1])
    forward_share(3)

    for d, i, j in ((3, 0, 2), (1, 1, 3), (2, 4, 5)):
        for k in range(2):
            if d == 2:
                sixths[k, i].wait_recv()
            sixths[k, j].wait_recv()
            to_sibling(beside(k, d), 4 * k + d)
    for n in range(4):
        for k in range(2):
            second_y[n, k].wait_recv()
        tgrad_ref[:, n * 256:(n + 1) * 256] = (SCALE * (hacc[0:R, n * 256:(n + 1) * 256] + g_in[n].astype(F32))).astype(BF16)
    write(tgrad_ref, tgrad_out, 16)

    for copy, (p, k) in zip(lasts, blocks):
        copy.wait_recv()
        rows = pl.ds(pl.multiple_of((1 - c) * 640 + p * 80, 16), 80)
        write(pg_ref.at[rows], pg_out.at[rows], 8 + k)
    for copy in written:
        copy.wait()
    for copy in started:
        if not any(copy is other for other in passed_on):
            copy.wait_send()


def finish(loss_in, text_in, proj_in, loss_ref, text_ref, proj_ref):
    loss_ref[...] = loss_in[0, :]
    text_ref[...] = text_in[...]
    proj_ref[...] = proj_in[...].astype(F32)


def on_device(audio_emb, text_emb, proj_weight, pair_index):
    dma = pltpu.SemaphoreType.DMA
    hbm = pl.BlockSpec(memory_space=pl.ANY)
    vmem = pl.BlockSpec(memory_space=pltpu.VMEM)
    sems = []
    for shape in ((2, 6), (2, R // TR), (3, 2), (R // TR,), (2, 3), (4,), (2, 2, 4), (4,), (4, 2, 3), (2, 3), (7,), (7,), (2, 3), (2, 6), (8,)):
        sems += [dma(shape), dma(shape)]
    loss, text_grad, shares = pl.pallas_call(
        kernel,
        out_shape=(
            jax.ShapeDtypeStruct((1, R), F32),
            jax.ShapeDtypeStruct((R, E), BF16),
            jax.ShapeDtypeStruct((A, E), BF16),
        ),
        in_specs=[hbm, hbm, hbm, vmem],
        out_specs=(vmem, hbm, hbm),
        scratch_shapes=[
            pltpu.VMEM((4, R, A), BF16),
            pltpu.VMEM((4, A, R), BF16),
            pltpu.VMEM((A, E), BF16),
            pltpu.VMEM((R, E), BF16),
            pltpu.VMEM((2, R, E), BF16),
            pltpu.VMEM((R, E), BF16),
            pltpu.VMEM((2, 2, TR, E), BF16),
            pltpu.VMEM((4, R, E), BF16),
            pltpu.VMEM((2, 7 * R, HALF), F32),
            pltpu.VMEM((3, R, HALF), BF16),
            pltpu.VMEM((2, 4, R, HALF), BF16),
            pltpu.VMEM((2, 7, 1, HALF), F32),
            pltpu.VMEM((2, 7, 1, HALF), F32),
            pltpu.VMEM((2, 8, HALF), F32),
            pltpu.VMEM((2, 3, 8, HALF), F32),
            pltpu.VMEM((R, E), BF16),
            pltpu.VMEM((A, E), BF16),
            pltpu.VMEM((A, 3 * R), F32),
            pltpu.VMEM((A, 3 * R), BF16),
            pltpu.VMEM((4, R, 256), BF16),
            pltpu.VMEM((2, 4, R, 256), F32),
            pltpu.VMEM((4, R, 256), BF16),
            pltpu.VMEM((4, R, 256), BF16),
            pltpu.VMEM((4, 640, 256), BF16),
            pltpu.VMEM((4, 640, 256), BF16),
            pltpu.VMEM((4, 8, 80, 256), BF16),
            pltpu.VMEM((4, 2, 3, 80, 256), BF16),
            pltpu.VMEM((2, 4, 80, 256), F32),
            pltpu.VMEM((2, 4, 80, 256), BF16),
            pltpu.VMEM((2, 3, 80, 256), BF16),
            pltpu.VMEM((8, 3, 16, 128), F32),
            pltpu.VMEM((8, 3, 16, 128), BF16),
            pltpu.VMEM((7, 3, 16, 128), BF16),
            pltpu.VMEM((8, 3, 16, 128), BF16),
            dma((3,)),
            dma((17,)),
            *sems,
        ],
        compiler_params=pltpu.CompilerParams(
            collective_id=0, has_side_effects=True, vmem_limit_bytes=63 * 1024 * 1024
        ),
        cost_estimate=pl.CostEstimate(flops=24 * 10**9, bytes_accessed=16 * 2**20, transcendentals=4 * 2**20),
    )(audio_emb, text_emb, proj_weight, pair_index)
    return pl.pallas_call(
        finish,
        grid=(2,),
        out_shape=(
            jax.ShapeDtypeStruct((R,), F32),
            jax.ShapeDtypeStruct((R, E), BF16),
            jax.ShapeDtypeStruct((A, E), F32),
        ),
        in_specs=[
            pl.BlockSpec((1, R), lambda i: (0, 0)),
            pl.BlockSpec((R // 2, E), lambda i: (i, 0)),
            pl.BlockSpec((A // 2, E), lambda i: (i, 0)),
        ],
        out_specs=(
            pl.BlockSpec((R,), lambda i: (0,)),
            pl.BlockSpec((R // 2, E), lambda i: (i, 0)),
            pl.BlockSpec((A // 2, E), lambda i: (i, 0)),
        ),
        cost_estimate=pl.CostEstimate(flops=0, bytes_accessed=10 * 2**20, transcendentals=0),
    )(loss, text_grad, shares)


def solution(mesh):
    return jax.shard_map(
        on_device,
        mesh=mesh,
        in_specs=(P(("blk", "rep"), None), P(("blk", "rep"), None), P(), P(("blk", "rep"), None)),
        out_specs=(P(("blk", "rep")), P(("blk", "rep"), None), P()),
        check_vma=False,
    )
```

```python
import math

import jax
import jax.numpy as jnp
from jax import lax
from jax.experimental import pallas as pl
from jax.experimental.pallas import tpu as pltpu
from jax.sharding import PartitionSpec as P

A = 1280
E = 1024
R = 512
SCALE = 4.0 / math.sqrt(E)
NX, NY, NZ = 4, 4, 8
XR = 128
TR = 64
HALF = 256
NT = (((1,), (1,)), ((), ()))
F32 = jnp.float32
BF16 = jnp.bfloat16


def dot(a, b):
    return jnp.dot(a, b, preferred_element_type=F32)


def dot_nt(a, b):
    return lax.dot_general(a, b, NT, preferred_element_type=F32)


def part(i, size):
    return pl.ds(pl.multiple_of(i * size, size), size)


def kernel(
    aud_hbm, txt_hbm, w_hbm, pair_ref,
    loss_ref, tgrad_out, pg_out,
    aud, audt, w, txt, tadj, tfwd, tz, proj, sco, wt, wo, tops, totals, stat, stat_in,
    tgrad_ref, pg_ref, hacc, h, gz_in, gacc, gfwd, g_in,
    core_out, core_in, piece, in1, sum2, out2, in2, zown, zb, zin, zall,
    loc_sem, out_sem, xs, xr, ys, yr, es, er, zs, zr, ss, sr, gzs, gzr, gys, gyr,
    cs, cr, p1s, p1r, p2s, p2r, z1s, z1r, z2s, z2r, a2s, a2r, a1s, a1r, ks, kr,
):
    b = lax.axis_index("blk")
    rep = lax.axis_index("rep")
    x = lax.rem(b, NX)
    yh = lax.rem(lax.div(b, NX), 2)
    z = lax.div(b, NX * 2)
    c = lax.rem(rep, 2)
    y = yh * 2 + lax.div(rep, 2)

    def at(x_, y_, z_, c_):
        return ((z_ * 2 + lax.div(y_, 2)) * NX + x_, lax.rem(y_, 2) * 2 + c_)

    def x_peer(d):
        return at(lax.rem(x + d, NX), y, z, c)

    def y_peer(d):
        return at(x, lax.rem(y + d, NY), z, c)

    def z_peer(d):
        return at(x, y, lax.rem(z + d, NZ), c)

    sibling = at(x, y, z, 1 - c)
    step = 1 - 2 * yh
    z_next = at(x, y, lax.rem(z + step + NZ, NZ), c)
    z_back = at(x, y, lax.rem(z - step + NZ, NZ), c)

    started = []

    def remote(src, dst, s, r, device):
        return pltpu.make_async_remote_copy(
            src_ref=src, dst_ref=dst, send_sem=s, recv_sem=r,
            device_id=device, device_id_type=pl.DeviceIdType.MESH,
        )

    def send(src, dst, s, r, device):
        copy = remote(src, dst, s, r, device)
        copy.start()
        started.append(copy)
        return copy

    loads = [
        pltpu.make_async_copy(w_hbm, w, loc_sem.at[0]),
        pltpu.make_async_copy(aud_hbm, aud.at[0], loc_sem.at[1]),
        pltpu.make_async_copy(txt_hbm, txt, loc_sem.at[2]),
    ]
    for load in loads:
        load.start()

    barrier = pltpu.get_barrier_semaphore()
    peers = [x_peer(d) for d in range(1, NX)] + [y_peer(d) for d in range(1, NY)]
    peers += [z_peer(d) for d in range(1, NZ)] + [sibling]
    for peer in peers:
        pl.semaphore_signal(barrier, inc=1, device_id=peer, device_id_type=pl.DeviceIdType.MESH)
    pl.semaphore_wait(barrier, len(peers))

    right, left = x_peer(1), x_peer(3)
    up, down = y_peer(1), y_peer(3)
    rows_x = [pl.ds(i * XR, XR) for i in range(R // XR)]
    rows_t = [pl.ds(i * TR, TR) for i in range(R // TR)]
    n_up = R // TR // 2
    to_right, to_left, on_right, on_left = {}, {}, {}, {}
    to_up, to_down, on_up, on_down, on_z = {}, {}, {}, {}, {}

    def audio_out(half):
        i, j = 2 * half, 2 * half + 1
        for p, q in ((i, j), (j, i)):
            to_right[p] = send(aud_hbm.at[rows_x[p]], aud.at[1, rows_x[p]], xs.at[0, p], xr.at[0, p], right)
            to_left[q] = send(aud_hbm.at[rows_x[q]], aud.at[3, rows_x[q]], xs.at[1, q], xr.at[1, q], left)

    def audio_on(half):
        i, j = 2 * half, 2 * half + 1
        to_right[i].wait_recv()
        on_right[i] = send(aud.at[1, rows_x[i]], aud.at[2, rows_x[i]], xs.at[0, 4 + half], xr.at[0, 4 + half], right)
        to_left[j].wait_recv()
        on_left[j] = send(aud.at[3, rows_x[j]], aud.at[2, rows_x[j]], xs.at[1, 4 + half], xr.at[1, 4 + half], left)

    def text_out(i):
        k = n_up + i
        to_up[i] = send(txt_hbm.at[rows_t[i]], tfwd.at[rows_t[i]], ys.at[0, i], yr.at[0, i], up)
        to_down[k] = send(txt_hbm.at[rows_t[k]], tfwd.at[rows_t[k]], ys.at[0, k], yr.at[0, k], down)

    def text_on(i):
        k = n_up + i
        to_up[i].wait_recv()
        on_up[i] = send(tfwd.at[rows_t[i]], tadj.at[0, rows_t[i]], ys.at[1, i], yr.at[1, i], up)
        to_down[k].wait_recv()
        on_down[k] = send(tfwd.at[rows_t[k]], tadj.at[0, rows_t[k]], ys.at[1, k], yr.at[1, k], down)

    def text_z(i):
        k = n_up + i
        on_up[i].wait_recv()
        on_z[i] = send(tadj.at[0, rows_t[i]], tadj.at[1, rows_t[i]], zs.at[i], zr.at[i], z_next)
        on_down[k].wait_recv()
        on_z[k] = send(tadj.at[0, rows_t[k]], tadj.at[1, rows_t[k]], zs.at[k], zr.at[k], z_next)

    z_up, z_down = n_up - 1, 2 * n_up - 1
    ways = [(z_up, up), (z_down, down)]
    early, early_on, early_last = {}, {}, {}

    def early_out():
        for k, (i, _) in enumerate(ways):
            early[k] = send(txt_hbm.at[rows_t[i]], tz.at[0, k], es.at[0, k], er.at[0, k], z_back)

    def early_y():
        for k, (i, peer) in enumerate(ways):
            early[k].wait_recv()
            early_on[k] = send(tz.at[0, k], tz.at[1, k], es.at[1, k], er.at[1, k], peer)

    def early_end():
        for k, (i, peer) in enumerate(ways):
            early_on[k].wait_recv()
            early_last[k] = send(tz.at[1, k], tadj.at[1, rows_t[i]], es.at[2, k], er.at[2, k], peer)

    halves = [slice(0, HALF), slice(HALF, R)]

    def half(s):
        return part(s, HALF)

    def project(d, s):
        @pl.loop(0, 2)
        def _(n):
            cols = part(n, 512)
            proj[d, half(s), cols] = dot(aud[d, half(s), :], w[:, cols]).astype(BF16)

    def turn(d, s):
        @pl.loop(0, A // 128)
        def _(n):
            cols = part(n, 128)
            audt[d, cols, half(s)] = aud[d, half(s), cols].T

    def scores(s, index, text, d):
        @pl.loop(0, 2)
        def _(n):
            rows = pl.ds(pl.multiple_of(index * R + n * 256, 256), 256)
            sco[s, rows, :] = SCALE * dot_nt(text[part(n, 256), :], proj[d, half(s), :])

    def score_rows(index, n):
        return pl.ds(pl.multiple_of(index * R + n * 64, 64), 64)

    def exponents(s, index):
        def top_of(n, m):
            return jnp.maximum(m, jnp.max(sco[s, score_rows(index, n), :], axis=0, keepdims=True))

        m = lax.fori_loop(0, 8, top_of, jnp.full((1, HALF), -jnp.inf, F32))

        def total_of(n, t):
            e = jnp.exp(sco[s, score_rows(index, n), :] - m)
            sco[s, score_rows(index, n), :] = e
            return t + jnp.sum(e, axis=0, keepdims=True)

        tops[s, index] = m
        totals[s, index] = lax.fori_loop(0, 8, total_of, jnp.zeros((1, HALF), F32))

    def row_sums(s, d):
        m, t = tops[s, d], totals[s, d]
        if d > 0:
            m = jnp.maximum(m, tops[s, 3 + d])
            t = t * jnp.exp(tops[s, d] - m) + totals[s, 3 + d] * jnp.exp(tops[s, 3 + d] - m)
        stat[s, d:d + 1, :] = m
        stat[s, 4 + d:5 + d, :] = t

    def pair_scores(s):
        def block(n, paired):
            column = lax.broadcasted_iota(jnp.int32, (64, HALF), 0) + n * 64
            hot = (pair_ref[:, half(s)] == column).astype(F32)
            return paired + jnp.sum(sco[s, score_rows(0, n), :] * hot, axis=0, keepdims=True)

        loss_ref[:, half(s)] = lax.fori_loop(0, 8, block, jnp.zeros((1, HALF), F32))

    def sums_out(s):
        return [
            send(stat.at[s], stat_in.at[s, d - 1], ss.at[s, d - 1], sr.at[s, d - 1], x_peer(d))
            for d in range(1, NX)
        ]

    def log_sums(s):
        lse = []
        for d in range(NX):
            ms = [stat[s, d:d + 1, :]]
            ts = [stat[s, 4 + d:5 + d, :]]
            for back in range(1, NX):
                k = (d - back) % NX
                ms.append(stat_in[s, back - 1, k:k + 1, :])
                ts.append(stat_in[s, back - 1, 4 + k:5 + k, :])
            top = jnp.maximum(jnp.maximum(ms[0], ms[1]), jnp.maximum(ms[2], ms[3]))
            total = sum(t * jnp.exp(m - top) for m, t in zip(ms, ts))
            lse.append(top + jnp.log(total))
        return lse

    def weights(s, index, lse):
        factor = jnp.exp(tops[s, index] - lse)
        place = wt.at[index - 4] if index > 3 else wo.at[s, index]

        @pl.loop(0, 8)
        def _(n):
            place[part(n, 64), :] = (sco[s, score_rows(index, n), :] * factor).astype(BF16)

    def paired_weights(s, lse):
        factor = jnp.exp(tops[s, 0] - lse)

        @pl.loop(0, 8)
        def _(n):
            column = lax.broadcasted_iota(jnp.int32, (64, HALF), 0) + n * 64
            hot = (pair_ref[:, halves[s]] == column).astype(F32)
            wo[s, 0, part(n, 64), :] = (sco[s, score_rows(0, n), :] * factor - hot).astype(BF16)

        loss_ref[:, halves[s]] = lse - loss_ref[:, halves[s]]

    def via_z(d):
        return jnp.where(x >= d, 1 - yh, yh)

    zf = [None] + [via_z(d).astype(F32) for d in range(1, NX)]

    def adjacent_shares(s, n, cols):
        to_s, to_z = None, None
        for d in range(1, NX):
            g = dot(wt[d - 1], proj[d, halves[s], cols])
            gz = zf[d] * g
            to_z = gz if to_z is None else to_z + gz
            to_s = g - gz if to_s is None else to_s + (g - gz)
        return to_s, to_z

    def own_share(cols):
        g = None
        for s in range(2):
            for d in range(NX):
                v = dot(wo[s, d], proj[d, halves[s], cols])
                g = v if g is None else g + v
        return g

    def products(s):
        @pl.loop(0, 4)
        def _(n):
            rows = part(lax.div(n, 2), 640)
            j = lax.rem(n, 2)
            texts = part(j, 256)

            def keep(k, v):
                cols = part(2 * k + j, 256)
                if s == 0:
                    hacc[rows, cols] = v
                else:
                    h[rows, cols] = (hacc[rows, cols] + v).astype(BF16)

            own = dot_nt(audt[0, rows, halves[s]], wo[s, 0, texts, :])
            for d in range(1, NX):
                own = own + dot_nt(audt[d, rows, halves[s]], wo[s, d, texts, :])
            keep(0, own)
            to_s, to_z = None, None
            for d in range(1, NX):
                v = dot_nt(audt[d, rows, halves[s]], wt[d - 1, texts, :])
                vz = zf[d] * v
                to_z = vz if to_z is None else to_z + vz
                to_s = v - vz if to_s is None else to_s + (v - vz)
            keep(1, to_s)
            keep(2, to_z)

    def own_scores(s, d):
        scores(s, d, txt, d)
        exponents(s, d)
        turn(d, s)

    def adjacent_scores(s, d):
        scores(s, 3 + d, tadj.at[via_z(d)], d)
        exponents(s, 3 + d)

    audio_out(0)
    text_out(0)
    early_out()
    text_out(1)
    loads[0].wait()
    loads[1].wait()
    loads[2].wait()

    @pl.loop(0, 2)
    def _(s):
        project(0, s)
        scores(s, 0, txt, 0)
        pair_scores(s)
        exponents(s, 0)
        turn(0, s)

    text_on(0)
    text_out(2)
    text_on(1)
    early_y()
    text_out(3)
    audio_on(0)
    audio_out(1)
    row_sums(0, 0)
    row_sums(1, 0)
    text_z(0)
    text_on(2)
    text_z(1)
    early_end()
    text_on(3)
    to_right[1].wait_recv()
    to_left[0].wait_recv()

    @pl.loop(0, 2)
    def _(n):
        project(2 * n + 1, 0)
        own_scores(0, 2 * n + 1)

    text_z(2)
    on_right[0].wait_recv()
    on_left[1].wait_recv()
    project(2, 0)
    own_scores(0, 2)
    audio_on(1)
    for copy in [*on_z.values(), *early_last.values(), on_up[n_up - 1], on_down[2 * n_up - 1]]:
        copy.wait_recv()

    @pl.loop(1, 4)
    def _(d):
        adjacent_scores(0, d)

    for d in range(1, NX):
        row_sums(0, d)
    sums = sums_out(0)
    to_right[3].wait_recv()
    to_left[2].wait_recv()

    @pl.loop(0, 2)
    def _(n):
        d = 2 * n + 1
        project(d, 1)
        own_scores(1, d)
        adjacent_scores(1, d)

    for copy in sums:
        copy.wait_recv()
    lse = log_sums(0)
    for d in range(1, NX):
        weights(0, 3 + d, lse[d])
        weights(0, d, lse[d])
    paired_weights(0, lse[0])

    @pl.loop(0, 4)
    def _(n):
        to_s, to_z = adjacent_shares(0, n, part(n, 256))
        gacc[0, n] = to_s
        gacc[1, n] = to_z

    on_right[2].wait_recv()
    on_left[3].wait_recv()
    project(2, 1)
    scores(1, 2, txt, 2)
    exponents(1, 2)
    adjacent_scores(1, 2)
    for d in range(1, NX):
        row_sums(1, d)
    sums = sums_out(1)
    products(0)
    turn(2, 1)
    for copy in sums:
        copy.wait_recv()
    lse = log_sums(1)
    for d in range(1, NX):
        weights(1, 3 + d, lse[d])
    passed_on = [*on_up.values(), *on_down.values()]
    for copy in passed_on:
        copy.wait_send()
    def share_z(n):
        return remote(tfwd.at[:, part(n, 256)], gz_in.at[n], gzs.at[n], gzr.at[n], z_back)

    def last_shares(first, last):
        @pl.loop(first, last)
        def _(n):
            to_s, to_z = adjacent_shares(1, n, part(n, 256))
            tfwd[:, part(n, 256)] = (gacc[1, n] + to_z).astype(BF16)
            gacc[0, n] = gacc[0, n] + to_s
            share_z(n).start()

    last_shares(0, 1)
    shares_z = [share_z(n) for n in range(4)]
    started.extend(shares_z)
    for d in range(1, NX):
        weights(1, d, lse[d])
    paired_weights(1, lse[0])
    products(1)

    def term_rows(which, n):
        rows = part(which, 640)
        cols = part(n, 256)
        return (
            dot(h[rows, 0:512], txt[:, cols])
            + dot(h[rows, 512:1024], tadj[0, :, cols])
            + dot(h[rows, 1024:1536], tadj[1, :, cols])
        )

    def spot(n, p):
        return pl.ds(pl.multiple_of(n * 640 + p * 80, 16), 80)

    def pair_copy(n):
        return remote(core_out.at[n], core_in.at[n], cs.at[n], cr.at[n], sibling)

    def beside(k, d):
        return lax.rem((x, y)[k] + d, NX) + 4 * k

    def first_copy(n, k, d):
        return remote(
            piece.at[n, beside(k, d)], in1.at[n, k, d - 1],
            p1s.at[n, k, d - 1], p1r.at[n, k, d - 1], (x_peer, y_peer)[k](d),
        )

    first_y, second_y = {}, {}
    sides = [(pl.ds(0, HALF), up), (pl.ds(HALF, HALF), down)]

    def pass_share(n):
        shares_z[n].wait_recv()
        cols = slice(n * 256, (n + 1) * 256)
        aud[0, :, cols] = (gacc[0, n] + gz_in[n].astype(F32)).astype(BF16)
        for k, (rows, peer) in enumerate(sides):
            first_y[n, k] = send(aud.at[0, rows, cols], gfwd.at[n, rows], gys.at[0, k, n], gyr.at[0, k, n], peer)

    def forward_share(n):
        for k, (rows, peer) in enumerate(sides):
            first_y[n, k].wait_recv()
            second_y[n, k] = send(gfwd.at[n, rows], g_in.at[n, rows], gys.at[1, k, n], gyr.at[1, k, n], peer)

    @pl.loop(0, 5)
    def _(n):
        @pl.when(n < 4)
        def _():
            core_out[n] = term_rows(1 - c, n).astype(BF16)
            pair_copy(n).start()

        @pl.when(n > 0)
        def _():
            sco[0, part(n - 1, 640), :] = term_rows(c, n - 1)
            pair_copy(n - 1).wait_recv()

            @pl.loop(0, 8)
            def _(p):
                v = sco[0, spot(n - 1, p), :] + core_in[n - 1, pl.ds(pl.multiple_of(p * 80, 16), 80), :].astype(F32)
                sco[0, spot(n - 1, p), :] = v
                piece[n - 1, p] = v.astype(BF16)

            for d in (2, 1, 3):
                for k in range(2):
                    first_copy(n - 1, k, d).start()

    firsts = [first_copy(n, k, d) for n in range(4) for k in range(2) for d in range(1, NX)]
    started.extend(firsts)
    started.extend(pair_copy(n) for n in range(4))
    last_shares(1, 4)
    pass_share(0)

    def own_gradient(first, last):
        @pl.loop(first, last)
        def _(n):
            cols = part(n, 256)
            hacc[0:R, cols] = own_share(cols)

    for copy in firsts:
        copy.wait_recv()
    mine = (x, 4 + y)
    for n in range(4):
        for k in range(2):
            v = sco[0, spot(n, mine[k]), :]
            for d in range(3):
                v = v + in1[n, k, d].astype(F32)
            sum2[k, n] = v
            out2[k, n] = v.astype(BF16)
    seconds = []
    for d in (2, 1, 3):
        xd, yd = lax.rem(x + d, NX), lax.rem(y + d, NY)
        seconds.append(send(out2.at[0, yd], in2.at[0, d - 1], p2s.at[0, d - 1], p2r.at[0, d - 1], y_peer(d)))
        seconds.append(send(out2.at[1, xd], in2.at[1, d - 1], p2s.at[1, d - 1], p2r.at[1, d - 1], x_peer(d)))
    pass_share(1)
    own_gradient(0, 1)
    for copy in seconds:
        copy.wait_recv()
    theirs = (y, x)
    tiles = [(k, i, j) for k in range(2) for i in range(5) for j in range(2)]
    for k in range(2):
        v = sum2[k, theirs[k]]
        for d in range(3):
            v = v + in2[k, d].astype(F32)
        for t, (k_, i, j) in enumerate(tiles):
            if k_ == k:
                tile = v[i * 16:(i + 1) * 16, j * 128:(j + 1) * 128]
                zown[t // 3, t % 3] = tile
                zb[t // 3, t % 3] = tile.astype(BF16)
    for t in range(20, 24):
        zown[t // 3, t % 3] = jnp.zeros((16, 128), F32)
        zb[t // 3, t % 3] = jnp.zeros((16, 128), BF16)
    thirds = []
    far_first = (4, 3, 5, 2, 6, 1, 7)
    for d in far_first:
        zd = lax.rem(z + d, NZ)
        thirds.append(send(zb.at[zd], zin.at[d - 1], z1s.at[d - 1], z1r.at[d - 1], z_peer(d)))
    forward_share(0)
    own_gradient(1, 3)
    for copy in thirds:
        copy.wait_recv()
    v = zown[z]
    for d in range(NZ - 1):
        v = v + zin[d].astype(F32)
    zall[z] = (v * (SCALE / 256.0)).astype(BF16)
    fourths = [send(zall.at[z], zall.at[z], z2s.at[d - 1], z2r.at[d - 1], z_peer(d)) for d in far_first]
    forward_share(1)
    pass_share(2)
    own_gradient(3, 4)
    for copy in fourths:
        copy.wait_recv()

    def block(p, rows=80, more=0):
        return pl.ds(pl.multiple_of(c * 640 + p * 80 + more, 16), rows)

    def columns(n, size=256, more=0):
        return pl.ds(pl.multiple_of(n * 256 + more, 128), size)

    for t, (k, i, j) in enumerate(tiles):
        pg_ref[block(mine[k], 16, 16 * i), columns(theirs[k], 128, 128 * j)] = zall[t // 3, t % 3]
    fifths = []
    for k in range(2):
        own = pg_ref.at[block(mine[k]), columns(theirs[k])]
        for d in (2, 1, 3):
            fifths.append(send(own, own, a2s.at[k, d - 1], a2r.at[k, d - 1], (y_peer, x_peer)[k](d)))
    pass_share(3)
    forward_share(2)
    for copy in fifths:
        copy.wait_recv()
    sixths, lasts, written, blocks = {}, [], [], []

    def write(src, dst, k):
        copy = pltpu.make_async_copy(src, dst, out_sem.at[k])
        copy.start()
        written.append(copy)

    def to_sibling(p, k):
        rows = pg_ref.at[block(p)]
        write(rows, pg_out.at[block(p)], k)
        blocks.append((p, k))
        lasts.append(send(rows, rows, ks.at[k], kr.at[k], sibling))

    low, high = pl.ds(0, 512), pl.ds(512, 512)

    def spread(k, i, p, cols, peer):
        rows = pg_ref.at[block(p), cols]
        sixths[k, i] = send(rows, rows, a1s.at[k, i], a1r.at[k, i], peer)

    ends = [(x_peer(1), x_peer(3)), (y_peer(1), y_peer(3))]
    for k in range(2):
        spread(k, 0, mine[k], low, ends[k][0])
        spread(k, 1, mine[k], high, ends[k][1])
    for k in range(2):
        spread(k, 2, mine[k], high, ends[k][0])
        spread(k, 3, mine[k], low, ends[k][1])
        to_sibling(mine[k], 4 * k)
    for k in range(2):
        sixths[k, 0].wait_recv()
        spread(k, 4, beside(k, 3), low, ends[k][0])
        sixths[k, 1].wait_recv()
        spread(k, 5, beside(k, 1), high, ends[k][1])
    forward_share(3)

    for d, i, j in ((3, 0, 2), (1, 1, 3), (2, 4, 5)):
        for k in range(2):
            if d == 2:
                sixths[k, i].wait_recv()
            sixths[k, j].wait_recv()
            to_sibling(beside(k, d), 4 * k + d)
    for n in range(4):
        for k in range(2):
            second_y[n, k].wait_recv()
        tgrad_ref[:, n * 256:(n + 1) * 256] = (SCALE * (hacc[0:R, n * 256:(n + 1) * 256] + g_in[n].astype(F32))).astype(BF16)
    write(tgrad_ref, tgrad_out, 16)

    for copy, (p, k) in zip(lasts, blocks):
        copy.wait_recv()
        rows = pl.ds(pl.multiple_of((1 - c) * 640 + p * 80, 16), 80)
        write(pg_ref.at[rows], pg_out.at[rows], 8 + k)
    for copy in written:
        copy.wait()
    for copy in started:
        if not any(copy is other for other in passed_on):
            copy.wait_send()


def finish(loss_in, text_in, proj_in, loss_ref, text_ref, proj_ref):
    loss_ref[...] = loss_in[0, :]
    text_ref[...] = text_in[...]
    proj_ref[...] = proj_in[...].astype(F32)


def on_device(audio_emb, text_emb, proj_weight, pair_index):
    dma = pltpu.SemaphoreType.DMA
    hbm = pl.BlockSpec(memory_space=pl.ANY)
    vmem = pl.BlockSpec(memory_space=pltpu.VMEM)
    sems = []
    for shape in ((2, 6), (2, R // TR), (3, 2), (R // TR,), (2, 3), (4,), (2, 2, 4), (4,), (4, 2, 3), (2, 3), (7,), (7,), (2, 3), (2, 6), (8,)):
        sems += [dma(shape), dma(shape)]
    loss, text_grad, shares = pl.pallas_call(
        kernel,
        out_shape=(
            jax.ShapeDtypeStruct((1, R), F32),
            jax.ShapeDtypeStruct((R, E), BF16),
            jax.ShapeDtypeStruct((A, E), BF16),
        ),
        in_specs=[hbm, hbm, hbm, vmem],
        out_specs=(vmem, hbm, hbm),
        scratch_shapes=[
            pltpu.VMEM((4, R, A), BF16),
            pltpu.VMEM((4, A, R), BF16),
            pltpu.VMEM((A, E), BF16),
            pltpu.VMEM((R, E), BF16),
            pltpu.VMEM((2, R, E), BF16),
            pltpu.VMEM((R, E), BF16),
            pltpu.VMEM((2, 2, TR, E), BF16),
            pltpu.VMEM((4, R, E), BF16),
            pltpu.VMEM((2, 7 * R, HALF), F32),
            pltpu.VMEM((3, R, HALF), BF16),
            pltpu.VMEM((2, 4, R, HALF), BF16),
            pltpu.VMEM((2, 7, 1, HALF), F32),
            pltpu.VMEM((2, 7, 1, HALF), F32),
            pltpu.VMEM((2, 8, HALF), F32),
            pltpu.VMEM((2, 3, 8, HALF), F32),
            pltpu.VMEM((R, E), BF16),
            pltpu.VMEM((A, E), BF16),
            pltpu.VMEM((A, 3 * R), F32),
            pltpu.VMEM((A, 3 * R), BF16),
            pltpu.VMEM((4, R, 256), BF16),
            pltpu.VMEM((2, 4, R, 256), F32),
            pltpu.VMEM((4, R, 256), BF16),
            pltpu.VMEM((4, R, 256), BF16),
            pltpu.VMEM((4, 640, 256), BF16),
            pltpu.VMEM((4, 640, 256), BF16),
            pltpu.VMEM((4, 8, 80, 256), BF16),
            pltpu.VMEM((4, 2, 3, 80, 256), BF16),
            pltpu.VMEM((2, 4, 80, 256), F32),
            pltpu.VMEM((2, 4, 80, 256), BF16),
            pltpu.VMEM((2, 3, 80, 256), BF16),
            pltpu.VMEM((8, 3, 16, 128), F32),
            pltpu.VMEM((8, 3, 16, 128), BF16),
            pltpu.VMEM((7, 3, 16, 128), BF16),
            pltpu.VMEM((8, 3, 16, 128), BF16),
            dma((3,)),
            dma((17,)),
            *sems,
        ],
        compiler_params=pltpu.CompilerParams(
            collective_id=0, has_side_effects=True, vmem_limit_bytes=63 * 1024 * 1024
        ),
        cost_estimate=pl.CostEstimate(flops=24 * 10**9, bytes_accessed=16 * 2**20, transcendentals=4 * 2**20),
    )(audio_emb, text_emb, proj_weight, pair_index)
    return pl.pallas_call(
        finish,
        grid=(2,),
        out_shape=(
            jax.ShapeDtypeStruct((R,), F32),
            jax.ShapeDtypeStruct((R, E), BF16),
            jax.ShapeDtypeStruct((A, E), F32),
        ),
        in_specs=[
            pl.BlockSpec((1, R), lambda i: (0, 0)),
            pl.BlockSpec((R // 2, E), lambda i: (i, 0)),
            pl.BlockSpec((A // 2, E), lambda i: (i, 0)),
        ],
        out_specs=(
            pl.BlockSpec((R,), lambda i: (0,)),
            pl.BlockSpec((R // 2, E), lambda i: (i, 0)),
            pl.BlockSpec((A // 2, E), lambda i: (i, 0)),
        ),
        cost_estimate=pl.CostEstimate(flops=0, bytes_accessed=10 * 2**20, transcendentals=0),
    )(loss, text_grad, shares)


def solution(mesh):
    return jax.shard_map(
        on_device,
        mesh=mesh,
        in_specs=(P(("blk", "rep"), None), P(("blk", "rep"), None), P(), P(("blk", "rep"), None)),
        out_specs=(P(("blk", "rep")), P(("blk", "rep"), None), P()),
        check_vma=False,
    )
```
